32 devices in a mesh: pipe: 2 (over x), expert: 16 (over z, y, core).
Axes of the slice: x: 2, y: 2, z: 4, core: 2. Of those that a mesh axis runs over, the one named last changes fastest.
Arguments:
- fwd_acts: bfloat16 [2, 1024, 3584], P('pipe', 'expert'), may hold values from -6 to 6
- fwd_routes: int32 [2, 1024, 2], P('pipe', 'expert'), may hold values from 0 to 3, all different within a row; in each aligned block of 64 rows (0 to 63, 64 to 127, ..., all dimensions but the last counted through in order) at most 40 rows name the same one
- fwd_gates: float32 [2, 1024, 2], P('pipe', 'expert'), may hold values from 0.25 to 1
- back_acts: bfloat16 [2, 1024, 3584], P('pipe', 'expert'), may hold values from -6 to 6
- back_routes: int32 [2, 1024, 2], P('pipe', 'expert'), may hold values from 0 to 3, all different within a row; in each aligned block of 64 rows (0 to 63, 64 to 127, ..., all dimensions but the last counted through in order) at most 40 rows name the same one
- back_gates: float32 [2, 1024, 2], P('pipe', 'expert'), may hold values from 0.25 to 1
- back_grads: bfloat16 [2, 1024, 3584], P('pipe', 'expert'), may hold values from -0.59765625 to 0.59765625
- w_up: bfloat16 [2, 16, 3584, 256], P('pipe', 'expert'), may hold values from -0.09375 to 0.09375
- w_down: bfloat16 [2, 16, 256, 3584], P('pipe', 'expert'), may hold values from -0.1875 to 0.1875
Outputs:
- fwd_next: bfloat16 [2, 1024, 3584], P('pipe', 'expert')
- back_next: bfloat16 [2, 1024, 3584], P('pipe', 'expert')
- grad_up: float32 [2, 16, 3584, 256], P('pipe', 'expert')
- grad_down: float32 [2, 16, 256, 3584], P('pipe', 'expert')
The draws below stay inside these ranges and needn't reach their ends.
Inputs may be any that keep to these rules, and one draw needn't show every extreme that they name: `fwd_routes`: in each aligned block of 64 rows of a section the 2 experts of a row differ, and each expert is named by at most 40 rows, by exactly 40 in some block. `back_routes`: as for fwd_routes.
All inputs are finite; a program needn't handle non-finite values.
Results may differ from the reference program's by a relative error of at most 0.005.
Values may be sent and summed in bfloat16 or wider, within the bound.
No kernel may reach another device: no remote copies, remote signals or barrier semaphores. Data moves between devices by JAX's collectives and lax.ppermute only.
A program may use at most 192 MiB of HBM per device.

```python
import math
import jax
import jax.numpy as jnp
import numpy as np
from jax import lax

D = 3584
FF = 1024
GROUP = 4
TOP = 2
TOK = 64
FP = 256
EXPERTS = 4
CAP = 40
SECTIONS = 2
TOKENS = 1024
N_EXPERT = 16


def block_scale(stream_key, shape, pieces, smallest, top_value):
    loudness = 1.0
    for axis_at, parts in pieces:
        steps = jax.random.uniform(jax.random.fold_in(jax.random.fold_in(stream_key, 6), axis_at), (parts,), jnp.float32, smallest / len(pieces), top_value / len(pieces))
        loudness = loudness * jnp.repeat(jnp.exp(steps), shape[axis_at] // parts).reshape((-1,) + (1,) * (len(shape) - 1 - axis_at))
    return loudness


def deal_out(rng, own, number, rows, count, top, most, slope):
    ranking = jax.random.permutation(rng, count)
    heavy_load, ordinary = shares(count, rows * top, most, slope, True), shares(count, rows * top, most, slope, False)
    places = jnp.arange(count)

    def named(lengths, rotation):
        used = int((lengths > 0).sum())
        fixed = max(1, used // 4)
        moved = fixed + (places - fixed + rotation * (used - fixed)) % max(1, count - fixed)
        return jnp.zeros((count,), jnp.int32).at[ranking[jnp.where(places < fixed, places, moved)]].set(jnp.asarray(lengths, jnp.int32))

    lengths = jnp.where(number % 4 == 0, named(heavy_load, number // 4), named(ordinary, number - number // 4 - 1))
    mixed = jax.random.permutation(jax.random.fold_in(own, 3), count)
    source_of, taker = mixed[0:count // 2 * 2:2], mixed[1:count // 2 * 2:2]
    room = jnp.minimum(lengths[source_of] - 1, most - lengths[taker]) // 2
    room = jnp.where((source_of == ranking[0]) | (taker == ranking[0]) | (lengths[taker] == 0), 0, jnp.maximum(room, 0))
    moved = jax.random.randint(jax.random.fold_in(own, 4), (count // 2,), 0, 1 << 20) % (room + 1)
    lengths = lengths.at[source_of].add(-moved).at[taker].add(moved)
    items = jnp.searchsorted(jnp.cumsum(lengths), jnp.arange(rows * top), side="right").astype(jnp.int32)
    grid = items.reshape(top, rows).T
    grid = grid[jax.random.permutation(jax.random.fold_in(own, 1), rows)]
    rotation = jax.random.randint(jax.random.fold_in(own, 2), (rows, 1), 0, top)
    return jnp.take_along_axis(grid, (jnp.arange(top)[None, :] + rotation) % top, axis=1)


def shares(count, total, bound, slope, full):
    portions = [(1 << 20) // math.isqrt(rank ** slope) + 1 for rank in range(1, count + 1)]
    largest = bound if full else min(bound, max(-(-total // count), total * portions[0] // sum(portions)))
    least = 1 if total - largest >= count - 1 else 0
    holding, rest = [largest] + [least] * (count - 1), total - largest - least * (count - 1)
    while rest > 0:
        free = [i for i in range(1, count) if holding[i] < largest] or [i for i in range(1, count) if holding[i] < bound]
        mass, remaining = sum([portions[i] for i in free]), rest
        for i in free:
            extra = min(bound - holding[i], max(1, remaining * portions[i] // mass), rest)
            holding[i] = holding[i] + extra
            rest = rest - extra
    return np.array(holding)


def bell_draw(stream_key, extent, scale, bound, shards=(), held_as=jnp.bfloat16):
    result = scale * jax.random.normal(stream_key, extent, jnp.float32)
    if shards:
        result = result * block_scale(stream_key, extent, shards, -0.22, 0.18)
    return jnp.clip(result, -bound, bound).astype(held_as)


def setup_inputs(seed: int = 0) -> dict:
    seeds = jax.random.split(jax.random.key(seed), 10)
    fwd_acts = bell_draw(seeds[0], (SECTIONS, TOKENS, D), 1.0, 6.0, ((0, 2), (1, 16)))
    fwd_routes_keys = jax.random.split(jax.random.fold_in(seeds[1], 1), SECTIONS * TOKENS // TOK)
    fwd_routes_turns = jax.random.permutation(jax.random.fold_in(seeds[1], 3), SECTIONS * TOKENS // TOK)
    fwd_routes = jax.vmap(lambda own, number: deal_out(jax.random.fold_in(seeds[1], 2), own, number, TOK, EXPERTS, TOP, CAP, 1))(fwd_routes_keys, fwd_routes_turns).reshape((SECTIONS, TOKENS, TOP))
    fwd_gates = jnp.clip(0.25 + 0.75 * jax.random.uniform(seeds[2], (SECTIONS, TOKENS, TOP), jnp.float32) ** block_scale(seeds[2], (SECTIONS, TOKENS, TOP), ((0, 2), (1, 16)), -0.2, 0.2), 0.25, 1.0)
    back_acts = bell_draw(seeds[3], (SECTIONS, TOKENS, D), 1.0, 6.0, ((0, 2), (1, 16)))
    back_routes_keys = jax.random.split(jax.random.fold_in(seeds[4], 1), SECTIONS * TOKENS // TOK)
    back_routes_turns = jax.random.permutation(jax.random.fold_in(seeds[4], 3), SECTIONS * TOKENS // TOK)
    back_routes = jax.vmap(lambda own, number: deal_out(jax.random.fold_in(seeds[4], 2), own, number, TOK, EXPERTS, TOP, CAP, 1))(back_routes_keys, back_routes_turns).reshape((SECTIONS, TOKENS, TOP))
    back_gates = jnp.clip(0.25 + 0.75 * jax.random.uniform(seeds[5], (SECTIONS, TOKENS, TOP), jnp.float32) ** block_scale(seeds[5], (SECTIONS, TOKENS, TOP), ((0, 2), (1, 16)), -0.2, 0.2), 0.25, 1.0)
    back_grads = bell_draw(seeds[6], (SECTIONS, TOKENS, D), 0.1, 0.59765625, ((0, 2), (1, 16)))
    w_up = bell_draw(seeds[7], (SECTIONS, N_EXPERT, D, FP), D ** -0.5, 0.09375, ((0, 2), (1, 16)))
    w_down = bell_draw(seeds[8], (SECTIONS, N_EXPERT, FP, D), FF ** -0.5, 0.1875, ((0, 2), (1, 16)))
    return dict(fwd_acts=fwd_acts, fwd_routes=fwd_routes, fwd_gates=fwd_gates, back_acts=back_acts, back_routes=back_routes, back_gates=back_gates, back_grads=back_grads, w_up=w_up, w_down=w_down)


HIGH = lax.Precision.HIGHEST

def silu_grad(value):
    sigma = jax.nn.sigmoid(value)
    return sigma * (1.0 + value * (1.0 - sigma))

def tables(routes, gates):
    blocks, tok_rows, top_count = routes.shape
    flat = routes.reshape(blocks, tok_rows * top_count)
    onehot = (flat[:, :, None] == jnp.arange(EXPERTS, dtype=jnp.int32)[None, None, :]).astype(jnp.int32)
    before = jnp.cumsum(onehot, axis=1) - onehot
    slots = lax.optimization_barrier(jnp.sum(before * onehot, axis=2))
    places = (flat * CAP + slots).reshape(blocks, tok_rows, top_count)
    columns = jnp.arange(EXPERTS * CAP, dtype=jnp.int32)
    hits = (places[..., None] == columns).astype(jnp.float32)
    plain = lax.optimization_barrier(jnp.sum(hits, axis=2))
    gated = lax.optimization_barrier(jnp.sum(hits * gates[..., None], axis=2))
    return (plain, gated)

def dispatch(table, values):
    return jnp.einsum('jtc,jtd->jcd', table, values, precision=HIGH)

def by_expert(rows):
    return rows.reshape(N_EXPERT, EXPERTS, CAP, D).transpose(1, 0, 2, 3).reshape(EXPERTS, N_EXPERT * CAP, D)

def by_block(rows):
    return rows.reshape(EXPERTS, N_EXPERT, CAP, D).transpose(1, 0, 2, 3).reshape(N_EXPERT, EXPERTS * CAP, D)

def expert_forward(operands):
    rows, up_slices, down_slices = operands
    full_up = up_slices.transpose(1, 0, 2).reshape(D, FF).astype(jnp.float32)
    pre = jnp.dot(rows.astype(jnp.float32), full_up, precision=HIGH)
    act = jax.nn.silu(pre).astype(jnp.bfloat16)
    total = jnp.zeros((rows.shape[0], D), jnp.float32)
    for member in range(GROUP):
        part = jnp.dot(act[:, member * FP:(member + 1) * FP].astype(jnp.float32), down_slices[member].astype(jnp.float32), precision=HIGH).astype(jnp.bfloat16)
        total = total + lax.optimization_barrier(part).astype(jnp.float32)
    return total

def expert_backward(operands):
    rows, grad_rows, up_slices, down_slices = operands
    full_up = up_slices.transpose(1, 0, 2).reshape(D, FF).astype(jnp.float32)
    full_down = down_slices.reshape(FF, D).astype(jnp.float32)
    rows_wide = rows.astype(jnp.float32)
    grads_wide = grad_rows.astype(jnp.float32)
    pre = jnp.dot(rows_wide, full_up, precision=HIGH)
    act = jax.nn.silu(pre).astype(jnp.bfloat16)
    dact = jnp.dot(grads_wide, full_down.T, precision=HIGH)
    dpre = (dact * silu_grad(pre)).astype(jnp.bfloat16)
    total = jnp.zeros((rows.shape[0], D), jnp.float32)
    for member in range(GROUP):
        part = jnp.dot(dpre[:, member * FP:(member + 1) * FP].astype(jnp.float32), up_slices[member].astype(jnp.float32).T, precision=HIGH).astype(jnp.bfloat16)
        total = total + lax.optimization_barrier(part).astype(jnp.float32)
    grad_up = jnp.dot(rows_wide.T, dpre.astype(jnp.float32), precision=HIGH)
    grad_up = grad_up.reshape(D, GROUP, FP).transpose(1, 0, 2)
    grad_down = jnp.dot(act.astype(jnp.float32).T, grads_wide, precision=HIGH).reshape(GROUP, FP, D)
    return (total, grad_up, grad_down)

def section(operands):
    fwd_in, fwd_rt, fwd_gt, back_in, back_rt, back_gt, back_dy, up_w, down_w = operands
    up_e = up_w.reshape(EXPERTS, GROUP, D, FP)
    down_e = down_w.reshape(EXPERTS, GROUP, FP, D)
    plain_f, gated_f = tables(fwd_rt.reshape(N_EXPERT, TOK, TOP), fwd_gt.reshape(N_EXPERT, TOK, TOP))
    inputs_f = fwd_in.reshape(N_EXPERT, TOK, D).astype(jnp.float32)
    rows_f = dispatch(plain_f, inputs_f).astype(jnp.bfloat16)
    outs_f = lax.map(expert_forward, (by_expert(rows_f), up_e, down_e))
    merged = jnp.einsum('jtc,jcd->jtd', gated_f, by_block(outs_f), precision=HIGH)
    section_out = (inputs_f + merged).astype(jnp.bfloat16).reshape(TOKENS, D)
    plain_b, gated_b = tables(back_rt.reshape(N_EXPERT, TOK, TOP), back_gt.reshape(N_EXPERT, TOK, TOP))
    inputs_b = back_in.reshape(N_EXPERT, TOK, D).astype(jnp.float32)
    grads_b = back_dy.reshape(N_EXPERT, TOK, D).astype(jnp.float32)
    rows_b = dispatch(plain_b, inputs_b).astype(jnp.bfloat16)
    rows_g = dispatch(gated_b, grads_b).astype(jnp.bfloat16)
    drows, grad_up, grad_down = lax.map(expert_backward, (by_expert(rows_b), by_expert(rows_g), up_e, down_e))
    spread_back = jnp.einsum('jtc,jcd->jtd', plain_b, by_block(drows), precision=HIGH)
    section_grad = (grads_b + spread_back).astype(jnp.bfloat16).reshape(TOKENS, D)
    return (section_out, section_grad, grad_up.reshape(N_EXPERT, D, FP), grad_down.reshape(N_EXPERT, FP, D))

def reference(fwd_acts, fwd_routes, fwd_gates, back_acts, back_routes, back_gates, back_grads, w_up, w_down):
    section_out, section_grad, grad_up, grad_down = lax.map(section, (fwd_acts, fwd_routes, fwd_gates, back_acts, back_routes, back_gates, back_grads, w_up, w_down))
    fwd_next = jnp.roll(section_out, 1, axis=0)
    back_next = jnp.roll(section_grad, -1, axis=0)
    return (fwd_next, back_next, grad_up, grad_down)
```

```python
import jax
import jax.numpy as jnp
from jax import lax
from jax.sharding import PartitionSpec as P

GROUP = 4
F32 = jnp.float32
BF16 = jnp.bfloat16


def after(value, *before):
    return lax.optimization_barrier((value, *before))[0]


def dot(left, right, contract):
    return lax.dot_general(left, right, ((contract[:1], contract[1:]), ((), ())), preferred_element_type=F32)


def local(
    fwd_acts, fwd_routes, fwd_gates, back_acts, back_routes, back_gates, back_grads, w_up, w_down
):
    devices = lax.axis_size("expert")
    sections = lax.axis_size("pipe")
    experts = devices // GROUP
    tok_rows, width = fwd_acts.shape[1:]
    top_count = fwd_routes.shape[2]
    cap = GROUP * (5 * tok_rows * top_count // (4 * devices))
    mine = lax.axis_index("expert") // GROUP

    def send(value, planes=0, flip=0, pipes=0):
        pairs = []
        for section in range(sections):
            for place in range(devices):
                target = (place // GROUP + planes) % experts * GROUP + (place % GROUP) ^ flip
                goal = (section + pipes) % sections * devices + target
                pairs.append((section * devices + place, goal))
        return lax.ppermute(value, ("pipe", "expert"), pairs)

    def tables(routes):
        nearby = (routes - mine) % experts
        flat = nearby.reshape(tok_rows * top_count)
        onehot = (flat[:, None] == jnp.arange(experts, dtype=jnp.int32)[None, :]).astype(jnp.int32)
        before = jnp.cumsum(onehot, axis=0) - onehot
        slots = jnp.sum(before * onehot, axis=1)
        places = (flat * cap + slots).reshape(tok_rows, top_count)
        columns = jnp.arange(experts * cap, dtype=jnp.int32)
        return (places[:, :, None] == columns).astype(BF16)

    def gather(hits, values):
        plain = jnp.sum(hits, axis=1)
        return [
            dot(plain[:, k * cap:(k + 1) * cap], values, (0, 0)).astype(BF16) for k in range(experts)
        ]

    fwd_input, back_input, out_grad = fwd_acts[0], back_acts[0], back_grads[0]
    up_own, down_own = w_up[0, 0], w_down[0, 0]

    up_y = send(up_own, flip=2)
    down_y = send(down_own, flip=2)
    up_c = send(up_own, flip=1)
    down_c = send(down_own, flip=1)
    up_d = send(up_y, flip=1)
    down_d = send(down_y, flip=1)

    hits_f = tables(fwd_routes[0])
    hits_b = tables(back_routes[0])
    gates_b = jnp.sum(hits_b.astype(F32) * back_gates[0][:, :, None], axis=(0, 1))

    f = gather(hits_f, fwd_input)
    got_f = [f[0]] + [send(f[k], planes=k) for k in range(1, experts)]
    x = gather(hits_b, back_input)
    got_x = [x[0]] + [send(after(x[k], got_f[k]), planes=k) for k in range(1, experts)]
    g = gather(hits_b, out_grad)
    g = [
        (g[k].astype(F32) * gates_b[k * cap:(k + 1) * cap, None]).astype(BF16) for k in range(experts)
    ]
    got_g = [g[0]] + [send(after(g[k], got_x[k]), planes=k) for k in range(1, experts)]

    res_f = send(fwd_input, pipes=1)
    res_hits_f = send(fwd_routes[0], pipes=1)
    res_gates = send(fwd_gates[0], pipes=1)
    res_b = send(out_grad, pipes=-1)
    res_hits_b = send(back_routes[0], pipes=-1)

    rows_f = jnp.concatenate(got_f, axis=0)
    rows_x = jnp.concatenate(got_x, axis=0)
    rows_g = jnp.concatenate(got_g, axis=0)

    up = jnp.concatenate([up_own, up_c, up_y, up_d], axis=1)
    down = jnp.concatenate([down_own, down_c, down_y, down_d], axis=0)

    act_f = jax.nn.silu(dot(rows_f, up, (1, 0))).astype(BF16)
    out_f = dot(act_f, down, (1, 0)).astype(BF16)

    pre = dot(rows_x, up, (1, 0))
    sigma = jax.nn.sigmoid(pre)
    act = (pre * sigma).astype(BF16)
    dact = dot(rows_g, down, (1, 1))
    dpre = (dact * sigma * (1.0 + pre * (1.0 - sigma))).astype(BF16)
    out_b = dot(dpre, up, (1, 1)).astype(BF16)

    hidden = up_own.shape[1]

    ret_f = [send(out_f[k * cap:(k + 1) * cap], planes=-k, pipes=1) for k in range(experts)]
    ret_b = [
        send(after(out_b[k * cap:(k + 1) * cap], ret_f[k]), planes=-k, pipes=-1)
        for k in range(experts)
    ]

    both = jnp.concatenate([act.reshape(-1, GROUP, hidden), dpre.reshape(-1, GROUP, hidden)], axis=2)
    both_all = [both[:, 0]] + [send(both[:, m], flip=m) for m in range(1, GROUP)]
    x_y = send(after(rows_x, up_y), flip=2)
    g_y = send(after(rows_g, down_y), flip=2)
    x_c, g_c = send(rows_x, flip=1), send(rows_g, flip=1)
    x_d, g_d = send(x_y, flip=1), send(g_y, flip=1)
    x_all = jnp.concatenate([rows_x, x_c, x_y, x_d], axis=0)
    g_all = jnp.concatenate([rows_g, g_c, g_y, g_d], axis=0)
    hid_all = jnp.concatenate(both_all, axis=0)
    grad_up = dot(x_all, hid_all[:, hidden:], (0, 0))
    grad_down = dot(hid_all[:, :hidden], g_all, (0, 0))

    def combine(residual, hits, gates, parts):
        total = residual.astype(F32)
        for choice in range(top_count):
            picked = dot(hits[:, choice], jnp.concatenate(parts, axis=0), (1, 0))
            total = total + (picked if gates is None else gates[:, choice:choice + 1] * picked)
        return total.astype(BF16)

    fwd_next = combine(res_f, tables(res_hits_f), res_gates, ret_f)
    back_next = combine(res_b, tables(res_hits_b), None, ret_b)
    return (fwd_next[None], back_next[None], grad_up[None, None], grad_down[None, None])


def solution(mesh):
    rows = P("pipe", "expert", None)
    slices = P("pipe", "expert", None, None)
    return jax.shard_map(
        local,
        mesh=mesh,
        in_specs=(rows,) * 7 + (slices,) * 2,
        out_specs=(rows, rows, slices, slices),
        check_vma=False,
    )
```

```python
import jax
import jax.numpy as jnp
from jax import lax
from jax.experimental import pallas as pl
from jax.experimental.pallas import tpu as pltpu
from jax.sharding import PartitionSpec as P

GROUP = 4
LANES = 128
F32 = jnp.float32
BF16 = jnp.bfloat16
VMEM = pl.BlockSpec(memory_space=pltpu.VMEM)
SMEM = pl.BlockSpec(memory_space=pltpu.SMEM)
ANY = pl.BlockSpec(memory_space=pl.ANY)
LIMIT = pltpu.CompilerParams(vmem_limit_bytes=12 * 2**20)


def after(values, *before):
    values = tuple(values)
    return lax.optimization_barrier((values, before))[0]


def dot(left, right, contract):
    return lax.dot_general(left, right, ((contract[:1], contract[1:]), ((), ())), preferred_element_type=F32)


def shape(*dims, dtype=BF16):
    return jax.ShapeDtypeStruct(dims, dtype)


def cost(gflops, mib):
    return pl.CostEstimate(flops=int(gflops * 1e9), bytes_accessed=mib * 2**20, transcendentals=0)


def build_kernel(
    experts, cap, mine_ref, fr_ref, fg_ref, br_ref, bg_ref, f_any, x_any, g_any, *refs
):
    outs, refs = refs[:experts], refs[experts:]
    table_f, table_b, f_ref, x_ref, g_ref, sems = refs
    copies = [
        pltpu.make_async_copy(src, dst, sems.at[i])
        for i, (src, dst) in enumerate(((f_any, f_ref), (x_any, x_ref), (g_any, g_ref)))
    ]
    for copy in copies:
        copy.start()
    tok_rows = f_ref.shape[0]
    wide = table_b.shape[2]
    mine = mine_ref[0]
    row = lax.broadcasted_iota(jnp.int32, (tok_rows, tok_rows), 0)
    col = lax.broadcasted_iota(jnp.int32, (tok_rows, tok_rows), 1)
    earlier = (row < col).astype(F32).astype(BF16)
    same = (row == col).astype(F32).astype(BF16)
    slot = lax.broadcasted_iota(jnp.int32, (cap, tok_rows), 0).astype(F32)
    at = [lax.rem(mine + k, experts) for k in range(experts)]

    def placed(routes, gates):
        named = [((routes[0:1] == e) | (routes[1:2] == e)).astype(F32) for e in at]
        gate = [jnp.where(routes[0:1] == e, gates[0:1], gates[1:2]) for e in at]
        rows = -(-experts // 16) * 16
        padded = jnp.concatenate(named + [jnp.zeros((rows - experts, tok_rows), F32)], axis=0)
        prefix = dot(padded.astype(BF16), earlier, (1, 0))
        hits = [jnp.where(prefix[k:k + 1] == slot, named[k], 0.0) for k in range(experts)]
        return hits, [hits[k] * gate[k] for k in range(experts)]

    def by_token(slots):
        rest = jnp.zeros((wide - experts * cap, tok_rows), F32)
        full = jnp.concatenate(slots + [rest], axis=0)
        return dot(same, full.astype(BF16), (1, 1)).astype(BF16)

    hits_f, gated_f = placed(fr_ref[...], fg_ref[...])
    hits_b, gated_b = placed(br_ref[...], bg_ref[...])
    for copy in copies:
        copy.wait()
    for k in range(experts):
        hits = hits_b[k].astype(BF16)
        rows_f = dot(hits_f[k].astype(BF16), f_ref[...], (1, 0))
        rows_x = dot(hits, x_ref[...], (1, 0))
        rows_g = dot(hits, g_ref[...], (1, 0)) * jnp.sum(gated_b[k], axis=1, keepdims=True)
        rows = jnp.concatenate([rows_f, rows_x, rows_g], axis=0)
        outs[k][...] = rows.astype(BF16)
    table_f[0] = by_token(gated_f)
    table_f[1] = by_token([part - part.astype(BF16).astype(F32) for part in gated_f])
    table_b[0] = by_token(hits_b)


def pack_kernel(side, up, down, packed):
    packed[:side] = down[...]
    for j in range(0, up.shape[0], side):
        packed[side:, j:j + side] = up[j:j + side]


def up_blocks(ref, side):
    width = max(ref.shape)
    if ref.shape[0] == width:
        return [ref[j:j + side] for j in range(0, width, side)]
    return [ref[side:, j:j + side] for j in range(0, width, side)]


def first_layer(rows_f, rows_x, rows_g, up, down):
    count, side = rows_f.shape[0], down.shape[0]
    rows = jnp.concatenate([rows_f[...], rows_x[...]], axis=0)
    if up.shape[1] == side:
        pre = dot(rows, up[...], (1, 0))
    else:
        pre = sum(
            dot(rows[:, j * side:(j + 1) * side], block, (1, 0))
            for j, block in enumerate(up_blocks(up, side))
        )
    sigma = 1.0 / (1.0 + jnp.exp(-pre))
    acts = (pre * sigma).astype(BF16)
    pre, sigma = pre[count:], sigma[count:]
    dact = dot(rows_g[...], down[...], (1, 1))
    dpre = (dact * (sigma * (1.0 + pre * (1.0 - sigma)))).astype(BF16)
    return acts[:count], acts[count:], dpre


def local(
    fwd_acts, fwd_routes, fwd_gates, back_acts, back_routes, back_gates, back_grads, w_up, w_down
):
    devices = lax.axis_size("expert")
    sections = lax.axis_size("pipe")
    experts = devices // GROUP
    tok_rows, width = fwd_acts.shape[1:]
    cap = GROUP * (5 * tok_rows * fwd_routes.shape[2] // (4 * devices))
    mine = lax.axis_index("expert") // GROUP
    hidden = w_up.shape[3]
    count = experts * cap
    wide = -(-count // LANES) * LANES
    tile = width // 7

    def send(value, planes=0, flip=0, pipes=0):
        pairs = []
        for section in range(sections):
            for place in range(devices):
                target = (place // GROUP + planes) % experts * GROUP + (place % GROUP ^ flip)
                goal = (section + pipes) % sections * devices + target
                pairs.append((section * devices + place, goal))
        return lax.ppermute(value, ("pipe", "expert"), pairs)

    fwd_input, back_input, out_grad = fwd_acts[0], back_acts[0], back_grads[0]
    up_own, down_own = w_up[0, 0], w_down[0, 0]
    away = range(1, experts)

    def both_ways(forth, back, planes=0):
        if sections == 2:
            parts = send(jnp.concatenate([forth, back], axis=0), planes=planes, pipes=1)
            return parts[:forth.shape[0]], parts[forth.shape[0]:]
        return send(forth, planes=planes, pipes=1), send(back, planes=planes, pipes=-1)

    up_c, down_c = send(up_own, flip=1), send(down_own, flip=1)
    packed_own = pl.pallas_call(
        lambda *refs: pack_kernel(hidden, *refs),
        out_shape=shape(2 * hidden, width),
        in_specs=[VMEM] * 2,
        out_specs=VMEM,
        name="pack",
        compiler_params=LIMIT,
        cost_estimate=cost(0, 8),
    )(up_own, down_own)
    built = pl.pallas_call(
        lambda *refs: build_kernel(experts, cap, *refs),
        out_shape=[shape(3 * cap, width)] * experts
        + [shape(2, tok_rows, wide), shape(1, tok_rows, wide)],
        in_specs=[SMEM] + [VMEM] * 4 + [ANY] * 3,
        out_specs=[VMEM] * (experts + 2),
        scratch_shapes=[pltpu.VMEM((tok_rows, width), BF16)] * 3 + [pltpu.SemaphoreType.DMA((3,))],
        name="build",
        compiler_params=LIMIT,
        cost_estimate=cost(1, 5),
    )(
        mine.reshape(1), fwd_routes[0].T, fwd_gates[0].T, back_routes[0].T, back_gates[0].T,
        fwd_input, back_input, out_grad,
    )
    table_f, table_b = built[experts:]

    tables = table_f.transpose(1, 0, 2).reshape(tok_rows, 2 * wide), jnp.concatenate([table_b[0]] * 2, axis=1)
    base_f = jnp.concatenate([fwd_input, tables[0]], axis=1)
    base_b = jnp.concatenate([out_grad, tables[1]], axis=1)
    *rows_out, packed_own, base_f, base_b = after([*built[1:experts], packed_own, base_f, base_b], up_c, down_c)
    got = [built[0]] + [send(rows_out[k - 1], planes=k) for k in away]
    packed_y = send(packed_own, flip=2)
    base_f, base_b = both_ways(base_f, base_b)
    packed_d = send(packed_y, flip=1)

    rows_f, rows_x, rows_g = (
        jnp.concatenate([part[i * cap:(i + 1) * cap] for part in got], axis=0) for i in range(3)
    )
    (rows_f,) = after([rows_f], base_f, base_b)

    def own_kernel(rows_f, rows_x, rows_g, *refs):
        weights, outs = refs[:4], refs[4:]
        for q in range(2):
            for out, value in zip(outs, first_layer(rows_f, rows_x, rows_g, *weights[2 * q:2 * q + 2])):
                out[:, q * hidden:(q + 1) * hidden] = value

    act_f01, act_b01, dpre01 = pl.pallas_call(
        own_kernel,
        out_shape=[shape(count, 2 * hidden)] * 3,
        in_specs=[VMEM] * 7,
        out_specs=[VMEM] * 3,
        name="own",
        compiler_params=LIMIT,
        cost_estimate=cost(2, 12),
    )(rows_f, rows_x, rows_g, up_own, down_own, up_c, down_c)

    def near_kernel(rows_f, rows_x, rows_g, weights, *outs):
        for out, value in zip(outs, first_layer(rows_f, rows_x, rows_g, weights, weights.at[:hidden])):
            out[...] = value

    act_f2, act_b2, dpre2 = pl.pallas_call(
        near_kernel,
        out_shape=[shape(count, hidden)] * 3,
        in_specs=[VMEM] * 4,
        out_specs=[VMEM] * 3,
        name="near",
        compiler_params=LIMIT,
        cost_estimate=cost(1, 6),
    )(rows_f, rows_x, rows_g, packed_y)

    def back_kernel(rows_f, rows_x, rows_g, act_b01, act_b2, dpre01, dpre2, up_own, up_c, packed_y, packed_d, *outs):
        out, act_f, sent, hid_own, hid_c = outs
        acts = first_layer(rows_f, rows_x, rows_g, packed_d, packed_d.at[:hidden])
        act_f[...] = acts[0]
        act_b = [act_b01[:, :hidden], act_b01[:, hidden:], act_b2[...], acts[1]]
        dpre = [dpre01[:, :hidden], dpre01[:, hidden:], dpre2[...], acts[2]]
        blocks = [up_blocks(ref, hidden) for ref in (up_own, up_c, packed_y, packed_d)]
        for j in range(width // hidden):
            out[:, j * hidden:(j + 1) * hidden] = sum(
                dot(dpre[q], blocks[q][j], (1, 1)) for q in range(GROUP)
            ).astype(BF16)
        sent[:, :width] = rows_g[...]
        for q in range(GROUP):
            target, low = [(hid_own, 0), (hid_c, 0), (sent, width), (sent, width + 2 * hidden)][q]
            target[:, low:low + hidden] = act_b[q]
            target[:, low + hidden:low + 2 * hidden] = dpre[q]

    out_b, act_f3, sent, hid_own, hid_c = pl.pallas_call(
        back_kernel,
        out_shape=[
            shape(count, width), shape(count, hidden), shape(count, width + 4 * hidden),
            shape(count, 2 * hidden), shape(count, 2 * hidden),
        ],
        in_specs=[VMEM] * 11,
        out_specs=[VMEM] * 5,
        name="back",
        compiler_params=LIMIT,
        cost_estimate=cost(2.4, 16),
    )(rows_f, rows_x, rows_g, act_b01, act_b2, dpre01, dpre2, up_own, up_c, packed_y, packed_d)

    def forward_kernel(act01, act2, act3, down_own, down_c, packed_y, packed_d, out):
        acts = [act01[:, :hidden], act01[:, hidden:], act2[...], act3[...]]
        for start in range(0, width, tile):
            span = slice(start, start + tile)
            out[:, span] = sum(
                dot(acts[q], weights[:hidden, span], (1, 0))
                for q, weights in enumerate((down_own, down_c, packed_y, packed_d))
            ).astype(BF16)

    rows_late = after([rows_x, rows_g], packed_d)
    x_c, g_c = send(rows_late[0], flip=1), send(rows_late[1], flip=1)
    out_f = pl.pallas_call(
        forward_kernel,
        out_shape=shape(count, width),
        in_specs=[VMEM] * 7,
        out_specs=VMEM,
        name="forward",
        compiler_params=LIMIT,
        cost_estimate=cost(1.3, 12),
    )(*after([act_f01], out_b, x_c, g_c), act_f2, act_f3, down_own, down_c, packed_y, packed_d)

    ret_f, ret_b = zip(*[
        both_ways(out_f[k * cap:(k + 1) * cap], out_b[k * cap:(k + 1) * cap], -k) for k in range(experts)
    ])

    x_y = send(*after([rows_x], packed_y), flip=2)
    sent_y = send(*after([sent], x_y, out_f), flip=2)
    x_late, hid_late = after([x_y, hid_c], sent_y)
    x_d, hid_c = send(x_late, flip=1), send(hid_late, flip=1)
    sent_d = send(sent_y, flip=1)
    hid_y, hid_d = sent_y[:, width:width + 2 * hidden], sent_d[:, width + 2 * hidden:]
    x_all = jnp.concatenate([rows_x, x_c, x_y, x_d], axis=0)
    g_all = jnp.concatenate([rows_g, g_c, sent_y[:, :width], sent_d[:, :width]], axis=0)
    hid_all = jnp.concatenate([hid_own, hid_c, hid_y, hid_d], axis=0)
    grad_up = dot(x_all, hid_all[:, hidden:], (0, 0))
    grad_down = dot(hid_all[:, :hidden], g_all, (0, 0))

    def combine(pieces, base, *parts):
        def kernel(base, *refs):
            parts, out = refs[:-1], refs[-1]
            table = base[:, width:]
            for start in range(0, width, tile):
                span = slice(start, start + tile)
                total = base[:, span].astype(F32)
                for k, part in enumerate(parts):
                    for piece in range(pieces):
                        low = piece * wide + k * cap
                        total = total + dot(table[:, low:low + cap], part[:, span], (1, 0))
                out[:, span] = total.astype(BF16)

        return pl.pallas_call(
            kernel,
            out_shape=shape(tok_rows, width),
            in_specs=[VMEM] * (1 + len(parts)),
            out_specs=VMEM,
            name="combine",
            compiler_params=LIMIT,
            cost_estimate=cost(0.1, 2),
        )(base, *parts)

    base_f, base_b = after([base_f, base_b], grad_up, grad_down)
    fwd_next = combine(2, base_f, *ret_f)
    back_next = combine(1, base_b, *ret_b)
    return (fwd_next[None], back_next[None], grad_up[None, None], grad_down[None, None])


def solution(mesh):
    rows = P("pipe", "expert", None)
    slices = P("pipe", "expert", None, None)
    return jax.shard_map(
        local,
        mesh=mesh,
        in_specs=(rows,) * 7 + (slices,) * 2,
        out_specs=(rows, rows, slices, slices),
        check_vma=False,
    )
```

```python
import jax
import jax.numpy as jnp
from jax import lax
from jax.experimental import pallas as pl
from jax.experimental.pallas import tpu as pltpu
from jax.sharding import PartitionSpec as P

GROUP = 4
LANES = 128
F32 = jnp.float32
BF16 = jnp.bfloat16
VMEM = pl.BlockSpec(memory_space=pltpu.VMEM)
SMEM = pl.BlockSpec(memory_space=pltpu.SMEM)
HBM = pl.BlockSpec(memory_space=pltpu.HBM)


def after(values, *before):
    return list(lax.optimization_barrier((tuple(values), before))[0])


def dot(left, right, contract):
    return lax.dot_general(left, right, ((contract[:1], contract[1:]), ((), ())), preferred_element_type=F32)


def shape(*dims, dtype=BF16):
    return jax.ShapeDtypeStruct(dims, dtype)


def cost(gflops, mib):
    return pl.CostEstimate(flops=int(gflops * 1e9), bytes_accessed=int(mib * 2**20), transcendentals=0)


def start_copies(pairs, sems):
    copies = [pltpu.make_async_copy(src, dst, sems.at[i]) for i, (src, dst) in enumerate(pairs)]
    for copy in copies:
        copy.start()
    return copies


def build_kernel(
    experts, cap, joined, mine_ref, fr_ref, fg_ref, br_ref, bg_ref, f_any, x_any, g_any, *refs
):
    outs, tables, (f_ref, x_ref, g_ref, sems) = refs[:experts], refs[experts:-4], refs[-4:]
    copies = start_copies(((f_any, f_ref), (x_any, x_ref), (g_any, g_ref)), sems)
    tok_rows = f_ref.shape[0]
    wide = tables[0].shape[1] // 2
    mine = mine_ref[0]
    row = lax.broadcasted_iota(jnp.int32, (tok_rows, tok_rows), 0)
    col = lax.broadcasted_iota(jnp.int32, (tok_rows, tok_rows), 1)
    earlier = (row < col).astype(F32).astype(BF16)
    same = (row == col).astype(F32).astype(BF16)
    slot = lax.broadcasted_iota(jnp.int32, (cap, tok_rows), 0).astype(F32)
    at = [lax.rem(mine + k, experts) for k in range(experts)]

    def placed(routes, gates):
        named = [((routes[0:1] == e) | (routes[1:2] == e)).astype(F32) for e in at]
        gate = [jnp.where(routes[0:1] == e, gates[0:1], gates[1:2]) for e in at]
        rows = -(-experts // 16) * 16
        padded = jnp.concatenate(named + [jnp.zeros((rows - experts, tok_rows), F32)], axis=0)
        prefix = dot(padded.astype(BF16), earlier, (1, 0))
        hits = [jnp.where(prefix[k:k + 1] == slot, named[k], 0.0) for k in range(experts)]
        return hits, [hits[k] * gate[k] for k in range(experts)]

    def by_token(slots):
        filled = sum(part.shape[0] for part in slots)
        full = jnp.concatenate(slots + [jnp.zeros((wide - filled, tok_rows), F32)], axis=0)
        return dot(same, full.astype(BF16), (1, 1)).astype(BF16)

    hits_f, gated_f = placed(fr_ref[...], fg_ref[...])
    hits_b, gated_b = placed(br_ref[...], bg_ref[...])
    rest_f = [part - part.astype(BF16).astype(F32) for part in gated_f]
    empty = jnp.zeros((cap, tok_rows), F32)
    for copy in copies:
        copy.wait()
    for k in range(experts):
        hits = hits_b[k].astype(BF16)
        rows_f = dot(hits_f[k].astype(BF16), f_ref[...], (1, 0))
        rows_x = dot(hits, x_ref[...], (1, 0))
        rows_g = dot(hits, g_ref[...], (1, 0)) * jnp.sum(gated_b[k], axis=1, keepdims=True)
        outs[k][...] = jnp.concatenate([rows_f, rows_x, rows_g], axis=0).astype(BF16)

    if joined:
        slots_f = [[part for k in range(experts) for part in (parts[k], empty)] for parts in (gated_f, rest_f)]
        slots_b = [part for k in range(experts) for part in (empty, hits_b[k])]
        tops = ((tables[0], 0, slots_f), (tables[0], tok_rows, [slots_b, None]))
    else:
        tops = ((tables[0], 0, [gated_f, rest_f]), (tables[1], 0, [hits_b, None]))
    for table, low, slots in tops:
        for i, part in enumerate(slots):
            value = jnp.zeros((tok_rows, wide), BF16) if part is None else by_token(part)
            table[low:low + tok_rows, i * wide:(i + 1) * wide] = value


def silu_slope(pre):
    sigma = 1.0 / (1.0 + jnp.exp(-pre))
    return pre * sigma, sigma * (1.0 + pre * (1.0 - sigma))


def hidden_units(rows_f, rows_x, rows_g, weights):
    count = rows_f.shape[0]
    up, down = weights
    pre = dot(jnp.concatenate([rows_f[...], rows_x[...]], axis=0), up[...], (1, 0))
    act, slope = silu_slope(pre)
    dact = dot(rows_g[...], down[...], (1, 1))
    return act[:count].astype(BF16), (dact * slope[count:]).astype(BF16)


def own_kernel(rows_f, rows_x, rows_g, up, down, up_c, down_c, act_f, dpre):
    side = down.shape[0]
    for q, weights in enumerate(((up, down), (up_c, down_c))):
        cols = slice(q * side, (q + 1) * side)
        act_f[:, cols], dpre[:, cols] = hidden_units(rows_f, rows_x, rows_g, weights)


def near_kernel(rows_f, rows_x, rows_g, act_f, dpre, up, down, up_c, down_c, up_y, down_y, part_f, part_b):
    side = down.shape[0]
    last_act, last_dpre = hidden_units(rows_f, rows_x, rows_g, (up_y, down_y))
    acts = [act_f[:, :side], act_f[:, side:], last_act]
    dpres = [dpre[:, :side], dpre[:, side:], last_dpre]
    for j in range(0, part_f.shape[1], side):
        cols = slice(j, j + side)
        part_f[:, cols] = sum(dot(a, w[:, cols], (1, 0)) for a, w in zip(acts, (down, down_c, down_y)))
        part_b[:, cols] = sum(dot(d, w[cols, :], (1, 1)) for d, w in zip(dpres, (up, up_c, up_y)))


def far_kernel(cap, joined, rows_f, rows_x, rows_g, part_f, part_b, up, down, *outs):
    side = down.shape[0]
    act_f, dpre = hidden_units(rows_f, rows_x, rows_g, (up, down))
    experts = rows_f.shape[0] // cap
    for j in range(0, part_f.shape[1], side):
        cols = slice(j, j + side)
        out_f = part_f[:, cols] + dot(act_f, down[:, cols], (1, 0))
        out_b = part_b[:, cols] + dot(dpre, up[cols, :], (1, 1))
        for k in range(experts):
            rows = slice(k * cap, (k + 1) * cap)
            if joined:
                outs[k][:, cols] = jnp.concatenate([out_f[rows], out_b[rows]], axis=0).astype(BF16)
            else:
                outs[k][:, cols] = out_f[rows].astype(BF16)
                outs[experts + k][:, cols] = out_b[rows].astype(BF16)


def grads_kernel(xg_own, xg_c, xg_y, xg_d, own_up, own_down, grad_up, grad_down, up, down, sems):
    count = xg_own.shape[0] // 2
    side, width = down.shape
    all_x = [piece.at[:count] for piece in (xg_own, xg_c, xg_y, xg_d)]
    all_g = [piece.at[count:] for piece in (xg_own, xg_c, xg_y, xg_d)]
    acts, dpres = [], []
    for rows_x, rows_g in zip(all_x, all_g):
        act, slope = silu_slope(dot(rows_x[...], own_up[...], (1, 0)))
        acts.append(act.astype(BF16))
        dact = dot(rows_g[...], own_down[...], (1, 1))
        dpres.append((dact * slope).astype(BF16))
    act, dpre = jnp.concatenate(acts, axis=0), jnp.concatenate(dpres, axis=0)
    tile = 2 * side
    copies = []
    for t, low in enumerate(range(0, width, tile)):
        cols = slice(low, low + tile)
        up[cols, :] = dot(jnp.concatenate([rows[:, cols] for rows in all_x], axis=0), dpre, (0, 0))
        down[:, cols] = dot(act, jnp.concatenate([rows[:, cols] for rows in all_g], axis=0), (0, 0))
        span = pl.ds(low, tile)
        copies.append(pltpu.make_async_copy(up.at[span], grad_up.at[span], sems.at[0, t]))
        copies.append(pltpu.make_async_copy(down.at[:, span], grad_down.at[:, span], sems.at[1, t]))
        copies[-2].start()
        copies[-1].start()
    for copy in copies:
        copy.wait()


def combine_kernel(experts, count, tables, *refs):
    base, refs = refs[:count], refs[count:]
    whole, late, outs = refs[:experts], refs[experts:2 * experts - 1], refs[2 * experts - 1:]
    tokens, width = tables.shape[0], whole[0].shape[1]
    wide = tables.shape[1] // 2
    each = whole[0].shape[0]
    table = jnp.concatenate([tables[:, :wide], tables[:, wide:]], axis=0)
    pieces = [(0, whole[0])]
    for k in range(1, experts):
        pieces += [(k * each, whole[k]), (k * each + whole[k].shape[0], late[k - 1])]
    tile = width // 7
    for low in range(0, width, tile):
        cols = slice(low, low + tile)
        picked = sum(dot(table[:, at:at + part.shape[0]], part[:, cols], (1, 0)) for at, part in pieces)
        picked = picked[:tokens] + picked[tokens:]
        rows = tokens // count
        for i, out in enumerate(outs):
            out[:, cols] = (base[i][:, cols].astype(F32) + picked[i * rows:(i + 1) * rows]).astype(BF16)


def local(
    fwd_acts, fwd_routes, fwd_gates, back_acts, back_routes, back_gates, back_grads, w_up, w_down
):
    devices = lax.axis_size("expert")
    sections = lax.axis_size("pipe")
    experts = devices // GROUP
    tok_rows, width = fwd_acts.shape[1:]
    cap = GROUP * (5 * tok_rows * fwd_routes.shape[2] // (4 * devices))
    mine = lax.axis_index("expert") // GROUP
    hidden = w_up.shape[3]
    count = experts * cap
    joined = sections == 2
    each = 2 * cap if joined else cap
    wide = -(-experts * each // LANES) * LANES

    def send(value, planes=0, flip=0, pipes=0):
        pairs = []
        for section in range(sections):
            for place in range(devices):
                target = (place // GROUP + planes) % experts * GROUP + (place % GROUP ^ flip)
                goal = (section + pipes) % sections * devices + target
                pairs.append((section * devices + place, goal))
        return lax.ppermute(value, ("pipe", "expert"), pairs)

    def call(kernel, name, out_shape, inputs, estimate, limit=8, **more):
        return pl.pallas_call(
            kernel,
            out_shape=out_shape,
            in_specs=more.pop("in_specs", [VMEM] * len(inputs)),
            out_specs=more.pop("out_specs", [VMEM] * len(out_shape)),
            name=name,
            compiler_params=pltpu.CompilerParams(vmem_limit_bytes=limit * 2**20),
            cost_estimate=estimate,
            **more,
        )(*inputs)

    fwd_input, back_input, out_grad = fwd_acts[0], back_acts[0], back_grads[0]
    away = range(1, experts)

    up_own, down_own = w_up[0, 0], w_down[0, 0]
    up_c, down_c = send(up_own, flip=1), send(down_own, flip=1)
    up_y, down_y = send(up_own, flip=2), send(down_own, flip=2)
    res_f = send(fwd_input, pipes=1)
    tables = [shape(2 * tok_rows, 2 * wide)] if joined else [shape(tok_rows, 2 * wide)] * 2
    built = call(
        lambda *refs: build_kernel(experts, cap, joined, *refs),
        "build",
        [shape(3 * cap, width)] * experts + tables,
        (
            mine.reshape(1), fwd_routes[0].T, fwd_gates[0].T, back_routes[0].T, back_gates[0].T,
            fwd_input, back_input, out_grad,
        ),
        cost(100, 0.1),
        limit=56,
        in_specs=[SMEM] + [VMEM] * 4 + [HBM] * 3,
        scratch_shapes=[pltpu.VMEM((tok_rows, width), BF16)] * 3 + [pltpu.SemaphoreType.DMA((3,))],
    )
    rows_out, tables = built[:experts], built[experts:]
    got = [rows_out[0]] + after(rows_out[1:], up_c, down_c)
    got[-1:] = after(got[-1:], res_f)
    got[1:] = [send(part, planes=k) for k, part in enumerate(got[1:], 1)]
    up_d, down_d = send(up_y, flip=1), send(down_y, flip=1)
    out_grad, *tables = after([out_grad, *tables], up_d)
    res_b = send(out_grad, pipes=-1)
    tables = [send(table, pipes=1 - 2 * i) for i, table in enumerate(tables)]

    rows_f, rows_x, rows_g = (
        jnp.concatenate([part[i * cap:(i + 1) * cap] for part in got], axis=0) for i in range(3)
    )
    rows_xg = jnp.concatenate([rows_x, rows_g], axis=0)
    rows = rows_f, rows_x, rows_g = rows_f, rows_x, rows_g
    act_f, dpre = call(
        own_kernel, "own", [shape(count, 2 * hidden)] * 2, (*rows, up_own, down_own, up_c, down_c), cost(2, 12)
    )
    part_f, part_b = call(
        near_kernel,
        "near",
        [shape(count, width, dtype=F32)] * 2,
        (*rows, act_f, dpre, up_own, down_own, up_c, down_c, up_y, down_y),
        cost(3, 18),
    )
    outs = call(
        lambda *refs: far_kernel(cap, joined, *refs),
        "far",
        [shape(each, width)] * experts if joined else [shape(cap, width)] * (2 * experts),
        (*after(rows, res_b, *tables), part_f, part_b, up_d, down_d),
        cost(2, 10),
    )

    split = 4 * each // 5 // 16 * 16
    ways = range(2 * experts if not joined else experts)
    early = [outs[i] if i % experts == 0 else outs[i][:split] for i in ways]
    late = [None if i % experts == 0 else outs[i][split:] for i in ways]

    def back(value, i):
        return send(value, planes=-(i % experts), pipes=1 if i < experts else -1)

    ret = [back(early[i], i) for i in ways]
    ret_late = after([part for part in late if part is not None], *ret)
    ret_late = [back(part, i) for part, i in zip(ret_late, [i for i in ways if i % experts])]

    xg_y = send(*after([rows_xg], up_y, down_y), flip=2)
    xg_c = send(*after([rows_xg], up_d, down_d), flip=1)
    xg_d = send(*after([xg_y], *ret), flip=1)
    tiles = width // (2 * hidden)
    grad_up, grad_down = call(
        grads_kernel,
        "grads",
        [shape(width, hidden, dtype=F32), shape(hidden, width, dtype=F32)],
        (rows_xg, xg_c, xg_y, xg_d, up_own, down_own),
        cost(0.01, 0.1),
        limit=16,
        out_specs=[HBM] * 2,
        scratch_shapes=[
            pltpu.VMEM((width, hidden), F32), pltpu.VMEM((hidden, width), F32), pltpu.SemaphoreType.DMA((2, tiles)),
        ],
    )

    tables = after(tables, grad_up, grad_down)
    results = []
    bases = [(res_f, res_b)] if joined else [(res_f,), (res_b,)]
    for i, (base, table) in enumerate(zip(bases, tables)):
        parts = (*ret[i * experts:(i + 1) * experts], *ret_late[i * (experts - 1):(i + 1) * (experts - 1)])
        results += call(
            lambda *refs: combine_kernel(experts, len(base), *refs),
            "combine", [shape(tok_rows, width)] * (2 if joined else 1), (table, *base, *parts), cost(0.2, 4),
        )
    fwd_next, back_next = results
    return (fwd_next[None], back_next[None], grad_up[None, None], grad_down[None, None])


def solution(mesh):
    rows = P("pipe", "expert", None)
    slices = P("pipe", "expert", None, None)
    return jax.shard_map(
        local,
        mesh=mesh,
        in_specs=(rows,) * 7 + (slices,) * 2,
        out_specs=(rows, rows, slices, slices),
        check_vma=False,
    )
```

```python
import jax
import jax.numpy as jnp
from jax import lax
from jax.experimental import pallas as pl
from jax.experimental.pallas import tpu as pltpu
from jax.sharding import PartitionSpec as P

GROUP = 4
LANES = 128
F32 = jnp.float32
BF16 = jnp.bfloat16
VMEM = pl.BlockSpec(memory_space=pltpu.VMEM)
SMEM = pl.BlockSpec(memory_space=pltpu.SMEM)
HBM = pl.BlockSpec(memory_space=pltpu.HBM)


def after(values, *before):
    return list(lax.optimization_barrier((tuple(values), before))[0])


def dot(left, right, contract):
    return lax.dot_general(left, right, ((contract[:1], contract[1:]), ((), ())), preferred_element_type=F32)


def shape(*dims, dtype=BF16):
    return jax.ShapeDtypeStruct(dims, dtype)


def cost(gflops, mib):
    return pl.CostEstimate(flops=int(gflops * 1e9), bytes_accessed=int(mib * 2**20), transcendentals=0)


def start_copies(pairs, sems):
    copies = [pltpu.make_async_copy(src, dst, sems.at[i]) for i, (src, dst) in enumerate(pairs)]
    for copy in copies:
        copy.start()
    return copies


def build_kernel(
    experts, cap, joined, mine_ref, fr_ref, fg_ref, br_ref, bg_ref, f_any, x_any, g_any, *refs
):
    outs, tables, (f_ref, x_ref, g_ref, sems) = refs[:experts], refs[experts:-4], refs[-4:]
    copies = start_copies(((f_any, f_ref), (x_any, x_ref), (g_any, g_ref)), sems)
    tok_rows = f_ref.shape[0]
    wide = table_width(experts, 2 * cap if joined else cap)
    mine = mine_ref[0]
    row = lax.broadcasted_iota(jnp.int32, (tok_rows, tok_rows), 0)
    col = lax.broadcasted_iota(jnp.int32, (tok_rows, tok_rows), 1)
    earlier = (row < col).astype(F32).astype(BF16)
    same = (row == col).astype(F32).astype(BF16)
    slot = lax.broadcasted_iota(jnp.int32, (cap, tok_rows), 0).astype(F32)
    at = [lax.rem(mine + k, experts) for k in range(experts)]

    def placed(routes, gates):
        named = [((routes[0:1] == e) | (routes[1:2] == e)).astype(F32) for e in at]
        gate = [jnp.where(routes[0:1] == e, gates[0:1], gates[1:2]) for e in at]
        rows = -(-experts // 16) * 16
        padded = jnp.concatenate(named + [jnp.zeros((rows - experts, tok_rows), F32)], axis=0)
        prefix = dot(padded.astype(BF16), earlier, (1, 0))
        hits = [jnp.where(prefix[k:k + 1] == slot, named[k], 0.0) for k in range(experts)]
        return hits, [hits[k] * gate[k] for k in range(experts)]

    def by_token(slots):
        filled = sum(part.shape[0] for part in slots)
        full = jnp.concatenate(slots + [jnp.zeros((wide - filled, tok_rows), F32)], axis=0)
        return dot(same, full.astype(BF16), (1, 1)).astype(BF16)

    hits_f, gated_f = placed(fr_ref[...], fg_ref[...])
    hits_b, gated_b = placed(br_ref[...], bg_ref[...])
    rest_f = [part - part.astype(BF16).astype(F32) for part in gated_f]
    empty = jnp.zeros((cap, tok_rows), F32)
    for copy in copies:
        copy.wait()
    for k in range(experts):
        hits = hits_b[k].astype(BF16)
        rows_f = dot(hits_f[k].astype(BF16), f_ref[...], (1, 0))
        rows_x = dot(hits, x_ref[...], (1, 0))
        rows_g = dot(hits, g_ref[...], (1, 0)) * jnp.sum(gated_b[k], axis=1, keepdims=True)
        outs[k][...] = jnp.concatenate([rows_f, rows_x, rows_g], axis=0).astype(BF16)

    if joined:
        slots = [[part for k in range(experts) for part in (gated_f[k], hits_b[k])]]
        slots = [(tables[0], slots + [[part for k in range(experts) for part in (rest_f[k], empty)]])]
    else:
        slots = [(tables[0], [gated_f, rest_f]), (tables[1], [hits_b])]
    for table, parts in slots:
        for i, part in enumerate(parts):
            table[:, i * wide:(i + 1) * wide] = by_token(part)


def table_width(experts, each):
    return -(-experts * each // LANES) * LANES


def stage_kernel(*refs):
    for copy in start_copies(zip(refs[:4], refs[4:8]), refs[8]):
        copy.wait()


def silu_slope(pre):
    sigma = 1.0 / (1.0 + jnp.exp(-pre))
    return pre * sigma, sigma * (1.0 + pre * (1.0 - sigma))


def hidden_units(rows_f, rows_x, rows_g, weights):
    count = rows_f.shape[0]
    up, down = weights
    pre = dot(jnp.concatenate([rows_f[...], rows_x[...]], axis=0), up[...], (1, 0))
    act, slope = silu_slope(pre)
    dact = dot(rows_g[...], down[...], (1, 1))
    return act[:count].astype(BF16), (dact * slope[count:]).astype(BF16)


def own_kernel(rows_f, rows_x, rows_g, up, down, up_c, down_c, act_f, dpre):
    side = down.shape[0]
    for q, weights in enumerate(((up, down), (up_c, down_c))):
        cols = slice(q * side, (q + 1) * side)
        act_f[:, cols], dpre[:, cols] = hidden_units(rows_f, rows_x, rows_g, weights)


def near_kernel(rows_f, rows_x, rows_g, act_f, dpre, up, down, up_c, down_c, up_y, down_y, part_f, part_b):
    side = down.shape[0]
    last_act, last_dpre = hidden_units(rows_f, rows_x, rows_g, (up_y, down_y))
    acts = [act_f[:, :side], act_f[:, side:], last_act]
    dpres = [dpre[:, :side], dpre[:, side:], last_dpre]
    for j in range(0, part_f.shape[1], side):
        cols = slice(j, j + side)
        part_f[:, cols] = sum(dot(a, w[:, cols], (1, 0)) for a, w in zip(acts, (down, down_c, down_y)))
        part_b[:, cols] = sum(dot(d, w[cols, :], (1, 1)) for d, w in zip(dpres, (up, up_c, up_y)))


def far_kernel(cap, joined, rows_f, rows_x, rows_g, part_f, part_b, up, down, *outs):
    side = down.shape[0]
    act_f, dpre = hidden_units(rows_f, rows_x, rows_g, (up, down))
    experts = rows_f.shape[0] // cap
    for j in range(0, part_f.shape[1], side):
        cols = slice(j, j + side)
        out_f = part_f[:, cols] + dot(act_f, down[:, cols], (1, 0))
        out_b = part_b[:, cols] + dot(dpre, up[cols, :], (1, 1))
        for k in range(experts):
            rows = slice(k * cap, (k + 1) * cap)
            if joined:
                outs[k][:, cols] = jnp.concatenate([out_f[rows], out_b[rows]], axis=0).astype(BF16)
            else:
                outs[k][:, cols] = out_f[rows].astype(BF16)
                outs[experts + k][:, cols] = out_b[rows].astype(BF16)


def grads_kernel(xg_own, xg_c, xg_y, xg_d, own_up, own_down, grad_up, grad_down, up, down, sems):
    count = xg_own.shape[0] // 2
    side, width = down.shape
    all_x = [piece.at[:count] for piece in (xg_own, xg_c, xg_y, xg_d)]
    all_g = [piece.at[count:] for piece in (xg_own, xg_c, xg_y, xg_d)]
    acts, dpres = [], []
    for rows_x, rows_g in zip(all_x, all_g):
        act, slope = silu_slope(dot(rows_x[...], own_up[...], (1, 0)))
        acts.append(act.astype(BF16))
        dact = dot(rows_g[...], own_down[...], (1, 1))
        dpres.append((dact * slope).astype(BF16))
    act, dpre = jnp.concatenate(acts, axis=0), jnp.concatenate(dpres, axis=0)
    tile = 2 * side
    copies = []
    for t, low in enumerate(range(0, width, tile)):
        cols = slice(low, low + tile)
        up[cols, :] = dot(jnp.concatenate([rows[:, cols] for rows in all_x], axis=0), dpre, (0, 0))
        down[:, cols] = dot(act, jnp.concatenate([rows[:, cols] for rows in all_g], axis=0), (0, 0))
        span = pl.ds(low, tile)
        copies.append(pltpu.make_async_copy(up.at[span], grad_up.at[span], sems.at[0, t]))
        copies.append(pltpu.make_async_copy(down.at[:, span], grad_down.at[:, span], sems.at[1, t]))
        copies[-2].start()
        copies[-1].start()
    for copy in copies:
        copy.wait()


def picked_rows(experts, each, count, table, pieces, cols):
    tokens, wide = table.shape[0], table_width(experts, each)
    parts = [table[:, low:low + wide] for low in range(0, table.shape[1], wide)]
    if count == 2:
        forth = lax.broadcasted_iota(jnp.int32, (tokens, wide), 1) % each < each // 2
        parts = [jnp.where(forth, parts[0], 0), jnp.where(forth, 0, parts[0]), parts[1]]
    tables = jnp.concatenate(parts, axis=0)
    picked = sum(dot(tables[:, at:at + part.shape[0]], part[:, cols], (1, 0)) for at, part in pieces)
    total = picked[:count * tokens]
    if len(parts) > count:
        low = [picked[count * tokens:]]
        total = total + jnp.concatenate(low + [jnp.zeros((tokens, low[0].shape[1]), F32)] * (count - 1), axis=0)
    return total


def combine_first_kernel(each, count, table, *refs):
    base, whole, out = refs[:count], refs[count:-1], refs[-1]
    rows, width = base[0].shape
    pieces = [(k * each, part) for k, part in enumerate(whole)]
    for low in range(0, width, width // 7):
        cols = slice(low, low + width // 7)
        picked = picked_rows(len(whole), each, count, table, pieces, cols)
        for i in range(count):
            span = slice(i * rows, (i + 1) * rows)
            out[span, cols] = base[i][:, cols].astype(F32) + picked[span]


def combine_kernel(experts, each, at, table, total, late, *outs):
    rows, width = outs[0].shape
    for low in range(0, width, width // 7):
        cols = slice(low, low + width // 7)
        picked = total[:, cols] + picked_rows(experts, each, len(outs), table, [(at, late)], cols)
        for i, out in enumerate(outs):
            out[:, cols] = picked[i * rows:(i + 1) * rows].astype(BF16)


def local(
    fwd_acts, fwd_routes, fwd_gates, back_acts, back_routes, back_gates, back_grads, w_up, w_down
):
    devices = lax.axis_size("expert")
    sections = lax.axis_size("pipe")
    experts = devices // GROUP
    tok_rows, width = fwd_acts.shape[1:]
    cap = GROUP * (5 * tok_rows * fwd_routes.shape[2] // (4 * devices))
    mine = lax.axis_index("expert") // GROUP
    hidden = w_up.shape[3]
    count = experts * cap
    joined = sections == 2
    each = 2 * cap if joined else cap
    wide = table_width(experts, each)

    def send(value, planes=0, flip=0, pipes=0):
        pairs = []
        for section in range(sections):
            for place in range(devices):
                target = (place // GROUP + planes) % experts * GROUP + (place % GROUP ^ flip)
                goal = (section + pipes) % sections * devices + target
                pairs.append((section * devices + place, goal))
        return lax.ppermute(value, ("pipe", "expert"), pairs)

    def call(kernel, name, out_shape, inputs, estimate, limit=8, **more):
        return pl.pallas_call(
            kernel,
            out_shape=out_shape,
            in_specs=more.pop("in_specs", [VMEM] * len(inputs)),
            out_specs=more.pop("out_specs", [VMEM] * len(out_shape)),
            name=name,
            compiler_params=pltpu.CompilerParams(vmem_limit_bytes=limit * 2**20),
            cost_estimate=estimate,
            **more,
        )(*inputs)

    fwd_input, back_input, out_grad = fwd_acts[0], back_acts[0], back_grads[0]
    away = range(1, experts)

    up_own, down_own = w_up[0, 0], w_down[0, 0]
    up_c, down_c = send(up_own, flip=1), send(down_own, flip=1)
    up_y, down_y = send(up_own, flip=2), send(down_own, flip=2)
    res_f = send(fwd_input, pipes=1)
    tables = [shape(tok_rows, 2 * wide)] + ([] if joined else [shape(tok_rows, wide)])
    built = call(
        lambda *refs: build_kernel(experts, cap, joined, *refs),
        "build",
        [shape(3 * cap, width)] * experts + tables,
        (
            mine.reshape(1), fwd_routes[0].T, fwd_gates[0].T, back_routes[0].T, back_gates[0].T,
            fwd_input, back_input, out_grad,
        ),
        cost(100, 0.1),
        limit=56,
        in_specs=[SMEM] + [VMEM] * 4 + [HBM] * 3,
        scratch_shapes=[pltpu.VMEM((tok_rows, width), BF16)] * 3 + [pltpu.SemaphoreType.DMA((3,))],
    )
    rows_out, tables = built[:experts], built[experts:]
    got = [rows_out[0]] + after(rows_out[1:], up_c, down_c)
    got[-1:] = after(got[-1:], res_f)
    got[1:] = [send(part, planes=k) for k, part in enumerate(got[1:], 1)]
    res_b = send(out_grad, pipes=-1)
    tables = [send(table, pipes=1 - 2 * i) for i, table in enumerate(tables)]
    up_in, down_in, down_c, up_in_y = call(
        stage_kernel, "stage",
        [shape(width, hidden), shape(hidden, width), shape(hidden, width), shape(width, hidden)],
        after([up_own, down_own, down_c, up_y], res_b),
        cost(0.01, 0.1),
        limit=4,
        in_specs=[HBM] * 4,
        scratch_shapes=[pltpu.SemaphoreType.DMA((4,))],
    )
    up_d = send(up_y, flip=1)
    down_d = send(*after([down_y], up_in), flip=1)

    rows_f, rows_x, rows_g = (
        jnp.concatenate([part[i * cap:(i + 1) * cap] for part in got], axis=0) for i in range(3)
    )
    rows_xg = jnp.concatenate([rows_x, rows_g], axis=0)
    xg_c = send(rows_xg, flip=1)
    rows = rows_f, rows_x, rows_g = rows_f, rows_x, rows_g
    act_f, dpre = call(
        own_kernel, "own", [shape(count, 2 * hidden)] * 2, (*rows, up_in, down_in, up_c, down_c), cost(2, 12)
    )
    part_f, part_b = call(
        near_kernel,
        "near",
        [shape(count, width, dtype=F32)] * 2,
        (*rows, act_f, dpre, up_in, down_in, up_c, down_c, up_in_y, down_y),
        cost(3, 18),
    )
    outs = call(
        lambda *refs: far_kernel(cap, joined, *refs),
        "far",
        [shape(each, width)] * experts if joined else [shape(cap, width)] * (2 * experts),
        (*after(rows, xg_c, *tables), part_f, part_b, up_d, down_d),
        cost(2, 10),
    )

    middle = experts // 2
    split = max(3 * each // 5 // 16 * 16, each // 2)
    ways = range(len(outs))

    def back(value, i):
        return send(value, planes=-(i % experts), pipes=1 if i < experts else -1)

    ret = [back(outs[i][:split] if i % experts == middle else outs[i], i) for i in ways]
    ret_late = after([outs[i][split:] for i in ways if i % experts == middle], *ret)
    ret_late = [back(part, i * experts + middle) for i, part in enumerate(ret_late)]

    xg_y = send(*after([rows_xg], up_y, down_y), flip=2)
    xg_d = send(*after([xg_y], *ret), flip=1)
    bases = [(res_f, res_b)] if joined else [(res_f,), (res_b,)]
    totals = []
    for i, (base, table) in enumerate(zip(bases, tables)):
        totals += call(
            lambda *refs: combine_first_kernel(each, len(base), *refs),
            "combine_first",
            [shape(len(base) * tok_rows, width, dtype=F32)],
            (table, *base, *ret[i * experts:(i + 1) * experts]),
            cost(0.2, 4),
        )
    xg_d, *totals = after([xg_d, *totals])
    tiles = width // (2 * hidden)
    grad_up, grad_down = call(
        grads_kernel,
        "grads",
        [shape(width, hidden, dtype=F32), shape(hidden, width, dtype=F32)],
        (rows_xg, xg_c, xg_y, xg_d, up_in, down_in),
        cost(0.01, 0.1),
        limit=16,
        out_specs=[HBM] * 2,
        scratch_shapes=[
            pltpu.VMEM((width, hidden), F32), pltpu.VMEM((hidden, width), F32), pltpu.SemaphoreType.DMA((2, tiles)),
        ],
    )

    tables = after(tables, grad_up, grad_down)
    results = []
    for i, (table, total) in enumerate(zip(tables, totals)):
        results += call(
            lambda *refs: combine_kernel(experts, each, middle * each + split, *refs),
            "combine",
            [shape(tok_rows, width)] * len(bases[i]),
            (table, total, ret_late[i]),
            cost(0.1, 3),
        )
    fwd_next, back_next = results
    return (fwd_next[None], back_next[None], grad_up[None, None], grad_down[None, None])


def solution(mesh):
    rows = P("pipe", "expert", None)
    slices = P("pipe", "expert", None, None)
    return jax.shard_map(
        local,
        mesh=mesh,
        in_specs=(rows,) * 7 + (slices,) * 2,
        out_specs=(rows, rows, slices, slices),
        check_vma=False,
    )
```

```python
import jax
import jax.numpy as jnp
from jax import lax
from jax.experimental import pallas as pl
from jax.experimental.pallas import tpu as pltpu
from jax.sharding import PartitionSpec as P

GROUP = 4
LANES = 128
F32 = jnp.float32
BF16 = jnp.bfloat16
VMEM = pl.BlockSpec(memory_space=pltpu.VMEM)
SMEM = pl.BlockSpec(memory_space=pltpu.SMEM)
HBM = pl.BlockSpec(memory_space=pltpu.HBM)


def after(values, *before):
    return list(lax.optimization_barrier((tuple(values), before))[0])


def dot(left, right, contract):
    return lax.dot_general(left, right, ((contract[:1], contract[1:]), ((), ())), preferred_element_type=F32)


def shape(*dims, dtype=BF16):
    return jax.ShapeDtypeStruct(dims, dtype)


def cost(gflops, mib):
    return pl.CostEstimate(flops=int(gflops * 1e9), bytes_accessed=int(mib * 2**20), transcendentals=0)


def start_copies(pairs, sems):
    copies = [pltpu.make_async_copy(src, dst, sems.at[i]) for i, (src, dst) in enumerate(pairs)]
    for copy in copies:
        copy.start()
    return copies


def build_kernel(
    experts, cap, joined, mine_ref, fr_ref, fg_ref, br_ref, bg_ref, f_any, x_any, g_any, *refs
):
    outs, base_b, more, (f_ref, x_ref, g_ref, sems) = refs[:experts], refs[experts], refs[experts + 1:-4], refs[-4:]
    copies = start_copies(((f_any, f_ref), (x_any, x_ref), (g_any, g_ref)), sems)
    tok_rows = f_ref.shape[0]
    wide = table_width(experts, 2 * cap if joined else cap)
    mine = mine_ref[0]
    row = lax.broadcasted_iota(jnp.int32, (tok_rows, tok_rows), 0)
    col = lax.broadcasted_iota(jnp.int32, (tok_rows, tok_rows), 1)
    earlier = (row < col).astype(F32).astype(BF16)
    same = (row == col).astype(F32).astype(BF16)
    slot = lax.broadcasted_iota(jnp.int32, (cap, tok_rows), 0).astype(F32)
    at = [lax.rem(mine + k, experts) for k in range(experts)]

    def placed(routes, gates):
        named = [((routes[0:1] == e) | (routes[1:2] == e)).astype(F32) for e in at]
        gate = [jnp.where(routes[0:1] == e, gates[0:1], gates[1:2]) for e in at]
        rows = -(-experts // 16) * 16
        padded = jnp.concatenate(named + [jnp.zeros((rows - experts, tok_rows), F32)], axis=0)
        prefix = dot(padded.astype(BF16), earlier, (1, 0))
        hits = [jnp.where(prefix[k:k + 1] == slot, named[k], 0.0) for k in range(experts)]
        return hits, [hits[k] * gate[k] for k in range(experts)]

    def by_token(slots):
        filled = sum(part.shape[0] for part in slots)
        full = jnp.concatenate(slots + [jnp.zeros((wide - filled, tok_rows), F32)], axis=0)
        return dot(same, full.astype(BF16), (1, 1)).astype(BF16)

    hits_f, gated_f = placed(fr_ref[...], fg_ref[...])
    hits_b, gated_b = placed(br_ref[...], bg_ref[...])
    rest_f = [part - part.astype(BF16).astype(F32) for part in gated_f]
    empty = jnp.zeros((cap, tok_rows), F32)
    for copy in copies:
        copy.wait()
    for k in range(experts):
        hits = hits_b[k].astype(BF16)
        rows_f = dot(hits_f[k].astype(BF16), f_ref[...], (1, 0))
        rows_x = dot(hits, x_ref[...], (1, 0))
        rows_g = dot(hits, g_ref[...], (1, 0)) * jnp.sum(gated_b[k], axis=1, keepdims=True)
        outs[k][...] = jnp.concatenate([rows_f, rows_x, rows_g], axis=0).astype(BF16)

    width = f_ref.shape[1]
    base_b[:, :width] = g_ref[...]
    tables = [gated_f, rest_f]
    if joined:
        tables[0] = [part for k in range(experts) for part in (gated_f[k], hits_b[k])]
        tables[1] = [part for k in range(experts) for part in (rest_f[k], empty)]
    else:
        base_b[:, width:] = by_token(hits_b)
    for i, part in enumerate(tables):
        low = i * wide
        if joined:
            base_b[:, width + low:width + low + wide] = by_token(part)
        else:
            more[0][:, low:low + wide] = by_token(part)


def table_width(experts, each):
    return -(-experts * each // LANES) * LANES


def stage_kernel(*refs):
    half = len(refs) // 2
    for copy in start_copies(zip(refs[:half], refs[half:-1]), refs[-1]):
        copy.wait()


def silu_slope(pre):
    sigma = 1.0 / (1.0 + jnp.exp(-pre))
    return pre * sigma, sigma * (1.0 + pre * (1.0 - sigma))


def hidden_units(rows_f, rows_x, rows_g, weights):
    count = rows_f.shape[0]
    up, down = weights
    pre = dot(jnp.concatenate([rows_f[...], rows_x[...]], axis=0), up[...], (1, 0))
    act, slope = silu_slope(pre)
    dact = dot(rows_g[...], down[...], (1, 1))
    return act[:count].astype(BF16), (dact * slope[count:]).astype(BF16)


def own_kernel(rows_f, rows_x, rows_g, up, down, up_c, down_c, act_f, dpre):
    side = down.shape[0]
    for q, weights in enumerate(((up, down), (up_c, down_c))):
        cols = slice(q * side, (q + 1) * side)
        act_f[:, cols], dpre[:, cols] = hidden_units(rows_f, rows_x, rows_g, weights)


def near_kernel(rows_f, rows_x, rows_g, act_f, dpre, up, down, up_c, down_c, up_y, down_y, part_f, part_b):
    side = down.shape[0]
    last_act, last_dpre = hidden_units(rows_f, rows_x, rows_g, (up_y, down_y))
    acts = [act_f[:, :side], act_f[:, side:], last_act]
    dpres = [dpre[:, :side], dpre[:, side:], last_dpre]
    for j in range(0, part_f.shape[1], side):
        cols = slice(j, j + side)
        part_f[:, cols] = sum(dot(a, w[:, cols], (1, 0)) for a, w in zip(acts, (down, down_c, down_y)))
        part_b[:, cols] = sum(dot(d, w[cols, :], (1, 1)) for d, w in zip(dpres, (up, up_c, up_y)))


def far_kernel(cap, joined, rows_f, rows_x, rows_g, part_f, part_b, up, down, *outs):
    side = down.shape[0]
    act_f, dpre = hidden_units(rows_f, rows_x, rows_g, (up, down))
    experts = rows_f.shape[0] // cap
    for j in range(0, part_f.shape[1], side):
        cols = slice(j, j + side)
        out_f = part_f[:, cols] + dot(act_f, down[:, cols], (1, 0))
        out_b = part_b[:, cols] + dot(dpre, up[cols, :], (1, 1))
        for k in range(experts):
            rows = slice(k * cap, (k + 1) * cap)
            if joined:
                outs[k][:, cols] = jnp.concatenate([out_f[rows], out_b[rows]], axis=0).astype(BF16)
            else:
                outs[k][:, cols] = out_f[rows].astype(BF16)
                outs[experts + k][:, cols] = out_b[rows].astype(BF16)


def group_units(pieces, up, down):
    count = pieces[0].shape[0] // 2
    acts, dpres = [], []
    for piece in pieces:
        act, slope = silu_slope(dot(piece[:count], up[...], (1, 0)))
        dact = dot(piece[count:], down[...], (1, 1))
        acts.append(act.astype(BF16))
        dpres.append((dact * slope).astype(BF16))
    return jnp.concatenate(acts, axis=0), jnp.concatenate(dpres, axis=0)


def group_columns(pieces, cols):
    count = pieces[0].shape[0] // 2
    return [jnp.concatenate([piece[low:low + count, cols] for piece in pieces], axis=0) for low in (0, count)]


def chip_grads_kernel(xg_own, xg_c, own_up, own_down, up, down):
    pieces = (xg_own, xg_c)
    act, dpre = group_units(pieces, own_up, own_down)
    side, width = down.shape
    for low in range(0, width, 2 * side):
        cols = slice(low, low + 2 * side)
        rows_x, rows_g = group_columns(pieces, cols)
        up[cols, :] = dot(rows_x, dpre, (0, 0))
        down[:, cols] = dot(act, rows_g, (0, 0))


def grads_kernel(xg_y, xg_d, own_up, own_down, chip_up, chip_down, grad_up, grad_down, up, down, sems):
    pieces = (xg_y, xg_d)
    act, dpre = group_units(pieces, own_up, own_down)
    side, width = down.shape
    copies = []
    for t, low in enumerate(range(0, width, 2 * side)):
        cols = slice(low, low + 2 * side)
        rows_x, rows_g = group_columns(pieces, cols)
        up[cols, :] = chip_up[cols, :] + dot(rows_x, dpre, (0, 0))
        down[:, cols] = chip_down[:, cols] + dot(act, rows_g, (0, 0))
        span = pl.ds(low, 2 * side)
        copies.append(pltpu.make_async_copy(up.at[span], grad_up.at[span], sems.at[0, t]))
        copies.append(pltpu.make_async_copy(down.at[:, span], grad_down.at[:, span], sems.at[1, t]))
        copies[-2].start()
        copies[-1].start()
    for copy in copies:
        copy.wait()


def picked_rows(experts, each, count, table, pieces, cols):
    tokens, wide = table.shape[0], table_width(experts, each)
    parts = [table[:, low:low + wide] for low in range(0, table.shape[1], wide)]
    if count == 2:
        forth = lax.broadcasted_iota(jnp.int32, (tokens, wide), 1) % each < each // 2
        parts = [jnp.where(forth, parts[0], 0), jnp.where(forth, 0, parts[0]), parts[1]]
    tables = jnp.concatenate(parts, axis=0)
    picked = sum(dot(tables[:, at:at + part.shape[0]], part[:, cols], (1, 0)) for at, part in pieces)
    total = picked[:count * tokens]
    if len(parts) > count:
        low = [picked[count * tokens:]]
        total = total + jnp.concatenate(low + [jnp.zeros((tokens, low[0].shape[1]), F32)] * (count - 1), axis=0)
    return total


def combine_first_kernel(each, count, table, *refs):
    base, whole, out = refs[:count], refs[count:-1], refs[-1]
    rows, width = base[0].shape[0], out.shape[1]
    pieces = [(k * each, part) for k, part in enumerate(whole)]
    for low in range(0, width, width // 7):
        cols = slice(low, low + width // 7)
        picked = picked_rows(len(whole), each, count, table, pieces, cols)
        for i in range(count):
            span = slice(i * rows, (i + 1) * rows)
            out[span, cols] = base[i][:, cols].astype(F32) + picked[span]


def combine_kernel(experts, each, at, table, total, late, *outs):
    rows, width = outs[0].shape
    for low in range(0, width, width // 7):
        cols = slice(low, low + width // 7)
        picked = total[:, cols] + picked_rows(experts, each, len(outs), table, [(at, late)], cols)
        for i, out in enumerate(outs):
            out[:, cols] = picked[i * rows:(i + 1) * rows].astype(BF16)


def local(
    fwd_acts, fwd_routes, fwd_gates, back_acts, back_routes, back_gates, back_grads, w_up, w_down
):
    devices = lax.axis_size("expert")
    sections = lax.axis_size("pipe")
    experts = devices // GROUP
    tok_rows, width = fwd_acts.shape[1:]
    cap = GROUP * (5 * tok_rows * fwd_routes.shape[2] // (4 * devices))
    mine = lax.axis_index("expert") // GROUP
    hidden = w_up.shape[3]
    count = experts * cap
    joined = sections == 2
    each = 2 * cap if joined else cap
    wide = table_width(experts, each)

    def send(value, planes=0, flip=0, pipes=0):
        pairs = []
        for section in range(sections):
            for place in range(devices):
                target = (place // GROUP + planes) % experts * GROUP + (place % GROUP ^ flip)
                goal = (section + pipes) % sections * devices + target
                pairs.append((section * devices + place, goal))
        return lax.ppermute(value, ("pipe", "expert"), pairs)

    def call(kernel, name, out_shape, inputs, estimate, limit=8, **more):
        return pl.pallas_call(
            kernel,
            out_shape=out_shape,
            in_specs=more.pop("in_specs", [VMEM] * len(inputs)),
            out_specs=more.pop("out_specs", [VMEM] * len(out_shape)),
            name=name,
            compiler_params=pltpu.CompilerParams(vmem_limit_bytes=limit * 2**20),
            cost_estimate=estimate,
            **more,
        )(*inputs)

    fwd_input, back_input, out_grad = fwd_acts[0], back_acts[0], back_grads[0]
    away = range(1, experts)

    up_own, down_own = w_up[0, 0], w_down[0, 0]
    up_c, down_c = send(up_own, flip=1), send(down_own, flip=1)
    res_f = send(fwd_input, pipes=1)
    tables = [shape(tok_rows, width + 2 * wide)]
    if not joined:
        tables = [shape(tok_rows, width + wide), shape(tok_rows, 2 * wide)]
    built = call(
        lambda *refs: build_kernel(experts, cap, joined, *refs),
        "build",
        [shape(3 * cap, width)] * experts + tables,
        (
            mine.reshape(1), fwd_routes[0].T, fwd_gates[0].T, back_routes[0].T, back_gates[0].T,
            fwd_input, back_input, out_grad,
        ),
        cost(100, 0.1),
        limit=56,
        in_specs=[SMEM] + [VMEM] * 4 + [HBM] * 3,
        scratch_shapes=[pltpu.VMEM((tok_rows, width), BF16)] * 3 + [pltpu.SemaphoreType.DMA((3,))],
    )
    got, tables = list(built[:experts]), built[experts:]

    up_sent, down_sent = after([up_own, down_own], tables[0])
    up_y, down_y = send(up_sent, flip=2), send(down_sent, flip=2)
    base_b = send(tables[0], pipes=-1)
    table_f = None if joined else send(tables[1], pipes=1)
    got[1:] = after(got[1:], up_c, down_c)
    got[1:-1] = [send(part, planes=k) for k, part in enumerate(got[1:-1], 1)]
    up_in, down_in, down_c = call(
        stage_kernel, "stage",
        [shape(width, hidden), shape(hidden, width), shape(hidden, width)],
        (up_own, down_own, down_c),
        cost(0.01, 0.1),
        limit=4,
        in_specs=[HBM] * 3,
        scratch_shapes=[pltpu.SemaphoreType.DMA((3,))],
    )
    got[-1] = send(*after([got[-1]], up_in, res_f), planes=experts - 1)
    up_d = send(up_y, flip=1)
    down_d = send(*after([down_y], up_in, base_b), flip=1)

    rows_f, rows_x, rows_g = (
        jnp.concatenate([part[i * cap:(i + 1) * cap] for part in got], axis=0) for i in range(3)
    )
    rows_xg = jnp.concatenate([rows_x, rows_g], axis=0)
    xg_c = send(rows_xg, flip=1)
    rows = rows_f, rows_x, rows_g
    act_f, dpre = call(
        own_kernel, "own", [shape(count, 2 * hidden)] * 2, (*rows, up_in, down_in, up_c, down_c), cost(2, 12)
    )
    part_f, part_b = call(
        near_kernel,
        "near",
        [shape(count, width, dtype=F32)] * 2,
        (*rows, act_f, dpre, up_in, down_in, up_c, down_c, up_y, down_y),
        cost(3, 18),
    )
    outs = call(
        lambda *refs: far_kernel(cap, joined, *refs),
        "far",
        [shape(each, width)] * experts if joined else [shape(cap, width)] * (2 * experts),
        (*after(rows, xg_c), part_f, part_b, up_d, down_d),
        cost(2, 10),
    )

    middle = experts // 2
    split = 7 * each // 10 // 8 * 8
    ways = range(len(outs))

    def back(value, i):
        return send(value, planes=-(i % experts), pipes=1 if i < experts else -1)

    ret = [back(outs[i][:split] if i % experts == middle else outs[i], i) for i in ways]
    ret_late = after([outs[i][split:] for i in ways if i % experts == middle], *ret)
    ret_late = [back(part, i * experts + middle) for i, part in enumerate(ret_late)]

    xg_y = send(*after([rows_xg], up_y, down_y), flip=2)
    chip_up, chip_down = call(
        chip_grads_kernel,
        "chip_grads",
        [shape(width, hidden, dtype=F32), shape(hidden, width, dtype=F32)],
        (rows_xg, xg_c, up_in, down_in),
        cost(2, 10),
        limit=12,
    )
    xg_d = send(*after([xg_y], chip_up, chip_down, *ret), flip=1)
    tables = [base_b[:, width:]] if joined else [table_f, base_b[:, width:]]
    bases = [(res_f, base_b)] if joined else [(res_f,), (base_b,)]
    totals = []
    for i, (base, table) in enumerate(zip(bases, tables)):
        totals += call(
            lambda *refs: combine_first_kernel(each, len(base), *refs),
            "combine_first",
            [shape(len(base) * tok_rows, width, dtype=F32)],
            (table, *base, *ret[i * experts:(i + 1) * experts]),
            cost(0.2, 4),
        )
    xg_d, *totals = after([xg_d, *totals])
    tiles = width // (2 * hidden)
    grad_up, grad_down = call(
        grads_kernel,
        "grads",
        [shape(width, hidden, dtype=F32), shape(hidden, width, dtype=F32)],
        (xg_y, xg_d, up_in, down_in, chip_up, chip_down),
        cost(0.01, 0.1),
        limit=16,
        out_specs=[HBM] * 2,
        scratch_shapes=[
            pltpu.VMEM((width, hidden), F32), pltpu.VMEM((hidden, width), F32), pltpu.SemaphoreType.DMA((2, tiles)),
        ],
    )

    tables = after(tables, grad_up, grad_down)
    results = []
    for i, (table, total) in enumerate(zip(tables, totals)):
        results += call(
            lambda *refs: combine_kernel(experts, each, middle * each + split, *refs),
            "combine",
            [shape(tok_rows, width)] * len(bases[i]),
            (table, total, ret_late[i]),
            cost(0.1, 3),
        )
    fwd_next, back_next = results
    return (fwd_next[None], back_next[None], grad_up[None, None], grad_down[None, None])


def solution(mesh):
    rows = P("pipe", "expert", None)
    slices = P("pipe", "expert", None, None)
    return jax.shard_map(
        local,
        mesh=mesh,
        in_specs=(rows,) * 7 + (slices,) * 2,
        out_specs=(rows, rows, slices, slices),
        check_vma=False,
    )
```

```python
import jax
import jax.numpy as jnp
from jax import lax
from jax.experimental import pallas as pl
from jax.experimental.pallas import tpu as pltpu
from jax.sharding import PartitionSpec as P

GROUP = 4
LANES = 128
F32 = jnp.float32
BF16 = jnp.bfloat16
VMEM = pl.BlockSpec(memory_space=pltpu.VMEM)
SMEM = pl.BlockSpec(memory_space=pltpu.SMEM)
HBM = pl.BlockSpec(memory_space=pltpu.HBM)


def after(values, *before):
    return list(lax.optimization_barrier((tuple(values), before))[0])


def dot(left, right, contract):
    return lax.dot_general(left, right, ((contract[:1], contract[1:]), ((), ())), preferred_element_type=F32)


def shape(*dims, dtype=BF16):
    return jax.ShapeDtypeStruct(dims, dtype)


def cost(gflops, mib):
    return pl.CostEstimate(flops=int(gflops * 1e9), bytes_accessed=int(mib * 2**20), transcendentals=0)


def start_copies(pairs, sems):
    copies = [pltpu.make_async_copy(src, dst, sems.at[i]) for i, (src, dst) in enumerate(pairs)]
    for copy in copies:
        copy.start()
    return copies


def build_kernel(
    experts, cap, joined, mine_ref, fr_ref, fg_ref, br_ref, bg_ref, f_any, x_any, g_any, *refs
):
    outs, base_b, more, (f_ref, x_ref, g_ref, sems) = refs[:experts], refs[experts], refs[experts + 1:-4], refs[-4:]
    copies = start_copies(((f_any, f_ref), (x_any, x_ref), (g_any, g_ref)), sems)
    tok_rows = f_ref.shape[0]
    wide = table_width(experts, 2 * cap if joined else cap)
    mine = mine_ref[0]
    row = lax.broadcasted_iota(jnp.int32, (tok_rows, tok_rows), 0)
    col = lax.broadcasted_iota(jnp.int32, (tok_rows, tok_rows), 1)
    earlier = (row < col).astype(F32).astype(BF16)
    same = (row == col).astype(F32).astype(BF16)
    slot = lax.broadcasted_iota(jnp.int32, (cap, tok_rows), 0).astype(F32)
    at = [lax.rem(mine + k, experts) for k in range(experts)]

    def placed(routes, gates):
        named = [((routes[0:1] == e) | (routes[1:2] == e)).astype(F32) for e in at]
        gate = [jnp.where(routes[0:1] == e, gates[0:1], gates[1:2]) for e in at]
        rows = -(-experts // 16) * 16
        padded = jnp.concatenate(named + [jnp.zeros((rows - experts, tok_rows), F32)], axis=0)
        prefix = dot(padded.astype(BF16), earlier, (1, 0))
        hits = [jnp.where(prefix[k:k + 1] == slot, named[k], 0.0) for k in range(experts)]
        return hits, [hits[k] * gate[k] for k in range(experts)]

    def by_token(slots):
        filled = sum(part.shape[0] for part in slots)
        full = jnp.concatenate(slots + [jnp.zeros((wide - filled, tok_rows), F32)], axis=0)
        return dot(same, full.astype(BF16), (1, 1)).astype(BF16)

    hits_f, gated_f = placed(fr_ref[...], fg_ref[...])
    hits_b, gated_b = placed(br_ref[...], bg_ref[...])
    rest_f = [part - part.astype(BF16).astype(F32) for part in gated_f]
    empty = jnp.zeros((cap, tok_rows), F32)
    for copy in copies:
        copy.wait()
    for k in range(experts):
        hits = hits_b[k].astype(BF16)
        rows_f = dot(hits_f[k].astype(BF16), f_ref[...], (1, 0))
        rows_x = dot(hits, x_ref[...], (1, 0))
        rows_g = dot(hits, g_ref[...], (1, 0)) * jnp.sum(gated_b[k], axis=1, keepdims=True)
        outs[k][...] = jnp.concatenate([rows_f, rows_x, rows_g], axis=0).astype(BF16)

    width = f_ref.shape[1]
    base_b[:, :width] = g_ref[...]
    tables = [gated_f, rest_f]
    if joined:
        tables[0] = [part for k in range(experts) for part in (gated_f[k], hits_b[k])]
        tables[1] = [part for k in range(experts) for part in (rest_f[k], empty)]
    else:
        base_b[:, width:] = by_token(hits_b)
    for i, part in enumerate(tables):
        low = i * wide
        if joined:
            base_b[:, width + low:width + low + wide] = by_token(part)
        else:
            more[0][:, low:low + wide] = by_token(part)


def table_width(experts, each):
    return -(-experts * each // LANES) * LANES


def stage_kernel(*refs):
    half = len(refs) // 2
    for copy in start_copies(zip(refs[:half], refs[half:-1]), refs[-1]):
        copy.wait()


def silu_slope(pre):
    sigma = 1.0 / (1.0 + jnp.exp(-pre))
    return pre * sigma, sigma * (1.0 + pre * (1.0 - sigma))


def hidden_units(rows_f, rows_x, rows_g, weights):
    count = rows_f.shape[0]
    up, down = weights
    pre = dot(jnp.concatenate([rows_f[...], rows_x[...]], axis=0), up[...], (1, 0))
    act, slope = silu_slope(pre)
    dact = dot(rows_g[...], down[...], (1, 1))
    return act[:count].astype(BF16), (dact * slope[count:]).astype(BF16)


def own_kernel(rows_f, rows_x, rows_g, up, down, up_c, down_c, act_f, dpre):
    side = down.shape[0]
    for q, weights in enumerate(((up, down), (up_c, down_c))):
        cols = slice(q * side, (q + 1) * side)
        act_f[:, cols], dpre[:, cols] = hidden_units(rows_f, rows_x, rows_g, weights)


def near_kernel(rows_f, rows_x, rows_g, act_f, dpre, up, down, up_c, down_c, up_y, down_y, part_f, part_b):
    side = down.shape[0]
    last_act, last_dpre = hidden_units(rows_f, rows_x, rows_g, (up_y, down_y))
    acts = [act_f[:, :side], act_f[:, side:], last_act]
    dpres = [dpre[:, :side], dpre[:, side:], last_dpre]
    for j in range(0, part_f.shape[1], side):
        cols = slice(j, j + side)
        part_f[:, cols] = sum(dot(a, w[:, cols], (1, 0)) for a, w in zip(acts, (down, down_c, down_y)))
        part_b[:, cols] = sum(dot(d, w[cols, :], (1, 1)) for d, w in zip(dpres, (up, up_c, up_y)))


def far_kernel(cap, joined, rows_f, rows_x, rows_g, part_f, part_b, up, down, *outs):
    side = down.shape[0]
    act_f, dpre = hidden_units(rows_f, rows_x, rows_g, (up, down))
    experts = rows_f.shape[0] // cap
    for j in range(0, part_f.shape[1], side):
        cols = slice(j, j + side)
        out_f = part_f[:, cols] + dot(act_f, down[:, cols], (1, 0))
        out_b = part_b[:, cols] + dot(dpre, up[cols, :], (1, 1))
        for k in range(experts):
            rows = slice(k * cap, (k + 1) * cap)
            if joined:
                outs[k][:, cols] = jnp.concatenate([out_f[rows], out_b[rows]], axis=0).astype(BF16)
            else:
                outs[k][:, cols] = out_f[rows].astype(BF16)
                outs[experts + k][:, cols] = out_b[rows].astype(BF16)


def group_units(pieces, up, down):
    count = pieces[0].shape[0] // 2
    acts, dpres = [], []
    for piece in pieces:
        act, slope = silu_slope(dot(piece[:count], up[...], (1, 0)))
        dact = dot(piece[count:], down[...], (1, 1))
        acts.append(act.astype(BF16))
        dpres.append((dact * slope).astype(BF16))
    return jnp.concatenate(acts, axis=0), jnp.concatenate(dpres, axis=0)


def group_columns(pieces, cols):
    count = pieces[0].shape[0] // 2
    return [jnp.concatenate([piece[low:low + count, cols] for piece in pieces], axis=0) for low in (0, count)]


def chip_grads_kernel(xg_own, xg_c, own_up, own_down, up, down):
    pieces = (xg_own, xg_c)
    act, dpre = group_units(pieces, own_up, own_down)
    side, width = down.shape
    for low in range(0, width, 2 * side):
        cols = slice(low, low + 2 * side)
        rows_x, rows_g = group_columns(pieces, cols)
        up[cols, :] = dot(rows_x, dpre, (0, 0))
        down[:, cols] = dot(act, rows_g, (0, 0))


def grads_kernel(xg_y, xg_d, own_up, own_down, chip_up, chip_down, grad_up, grad_down, up, down, sems):
    pieces = (xg_y, xg_d)
    act, dpre = group_units(pieces, own_up, own_down)
    side, width = down.shape
    copies = []
    for t, low in enumerate(range(0, width, 2 * side)):
        cols = slice(low, low + 2 * side)
        rows_x, rows_g = group_columns(pieces, cols)
        up[cols, :] = chip_up[cols, :] + dot(rows_x, dpre, (0, 0))
        down[:, cols] = chip_down[:, cols] + dot(act, rows_g, (0, 0))
        span = pl.ds(low, 2 * side)
        copies.append(pltpu.make_async_copy(up.at[span], grad_up.at[span], sems.at[0, t]))
        copies.append(pltpu.make_async_copy(down.at[:, span], grad_down.at[:, span], sems.at[1, t]))
        copies[-2].start()
        copies[-1].start()
    for copy in copies:
        copy.wait()


def picked_rows(experts, each, count, table, pieces, cols):
    tokens, wide = table.shape[0], table_width(experts, each)
    parts = [table[:, low:low + wide] for low in range(0, table.shape[1], wide)]
    if count == 2:
        forth = lax.broadcasted_iota(jnp.int32, (tokens, wide), 1) % each < each // 2
        parts = [jnp.where(forth, parts[0], 0), jnp.where(forth, 0, parts[0]), parts[1]]
    tables = jnp.concatenate(parts, axis=0)
    picked = sum(dot(tables[:, at:at + part.shape[0]], part[:, cols], (1, 0)) for at, part in pieces)
    total = picked[:count * tokens]
    if len(parts) > count:
        low = [picked[count * tokens:]]
        total = total + jnp.concatenate(low + [jnp.zeros((tokens, low[0].shape[1]), F32)] * (count - 1), axis=0)
    return total


def combine_first_kernel(each, count, table, *refs):
    base, whole, out = refs[:count], refs[count:-1], refs[-1]
    rows, width = base[0].shape[0], out.shape[1]
    pieces = [(k * each, part) for k, part in enumerate(whole)]
    for low in range(0, width, width // 7):
        cols = slice(low, low + width // 7)
        picked = picked_rows(len(whole), each, count, table, pieces, cols)
        for i in range(count):
            span = slice(i * rows, (i + 1) * rows)
            out[span, cols] = base[i][:, cols].astype(F32) + picked[span]


def combine_kernel(experts, each, at, table, total, late, *outs):
    rows, width = outs[0].shape
    for low in range(0, width, width // 7):
        cols = slice(low, low + width // 7)
        picked = total[:, cols] + picked_rows(experts, each, len(outs), table, [(at, late)], cols)
        for i, out in enumerate(outs):
            out[:, cols] = picked[i * rows:(i + 1) * rows].astype(BF16)


def local(
    fwd_acts, fwd_routes, fwd_gates, back_acts, back_routes, back_gates, back_grads, w_up, w_down
):
    devices = lax.axis_size("expert")
    sections = lax.axis_size("pipe")
    experts = devices // GROUP
    tok_rows, width = fwd_acts.shape[1:]
    cap = GROUP * (5 * tok_rows * fwd_routes.shape[2] // (4 * devices))
    mine = lax.axis_index("expert") // GROUP
    hidden = w_up.shape[3]
    count = experts * cap
    joined = sections == 2
    each = 2 * cap if joined else cap
    wide = table_width(experts, each)

    def send(value, planes=0, flip=0, pipes=0):
        pairs = []
        for section in range(sections):
            for place in range(devices):
                target = (place // GROUP + planes) % experts * GROUP + (place % GROUP ^ flip)
                goal = (section + pipes) % sections * devices + target
                pairs.append((section * devices + place, goal))
        return lax.ppermute(value, ("pipe", "expert"), pairs)

    def call(kernel, name, out_shape, inputs, estimate, limit=8, **more):
        return pl.pallas_call(
            kernel,
            out_shape=out_shape,
            in_specs=more.pop("in_specs", [VMEM] * len(inputs)),
            out_specs=more.pop("out_specs", [VMEM] * len(out_shape)),
            name=name,
            compiler_params=pltpu.CompilerParams(vmem_limit_bytes=limit * 2**20),
            cost_estimate=estimate,
            **more,
        )(*inputs)

    fwd_input, back_input, out_grad = fwd_acts[0], back_acts[0], back_grads[0]
    away = range(1, experts)

    up_own, down_own = w_up[0, 0], w_down[0, 0]
    up_c, down_c = send(up_own, flip=1), send(down_own, flip=1)
    res_f = send(fwd_input, pipes=1)
    tables = [shape(tok_rows, width + 2 * wide)]
    if not joined:
        tables = [shape(tok_rows, width + wide), shape(tok_rows, 2 * wide)]
    built = call(
        lambda *refs: build_kernel(experts, cap, joined, *refs),
        "build",
        [shape(3 * cap, width)] * experts + tables,
        (
            mine.reshape(1), fwd_routes[0].T, fwd_gates[0].T, back_routes[0].T, back_gates[0].T,
            fwd_input, back_input, out_grad,
        ),
        cost(100, 0.1),
        limit=56,
        in_specs=[SMEM] + [VMEM] * 4 + [HBM] * 3,
        scratch_shapes=[pltpu.VMEM((tok_rows, width), BF16)] * 3 + [pltpu.SemaphoreType.DMA((3,))],
    )
    got, tables = list(built[:experts]), built[experts:]

    up_sent, down_sent = after([up_own, down_own], tables[0])
    up_y, down_y = send(up_sent, flip=2), send(down_sent, flip=2)
    base_b = send(tables[0], pipes=-1)
    table_f = None if joined else send(tables[1], pipes=1)
    got[1:] = after(got[1:], up_c, down_c)
    got[1:-1] = [send(part, planes=k) for k, part in enumerate(got[1:-1], 1)]
    up_in, down_in, down_c = call(
        stage_kernel, "stage",
        [shape(width, hidden), shape(hidden, width), shape(hidden, width)],
        (up_own, down_own, down_c),
        cost(0.01, 0.1),
        limit=4,
        in_specs=[HBM] * 3,
        scratch_shapes=[pltpu.SemaphoreType.DMA((3,))],
    )
    got[-1] = send(*after([got[-1]], up_in, res_f), planes=experts - 1)
    up_d = send(up_y, flip=1)
    down_d = send(*after([down_y], up_in, base_b), flip=1)

    rows_f, rows_x, rows_g = (
        jnp.concatenate([part[i * cap:(i + 1) * cap] for part in got], axis=0) for i in range(3)
    )
    rows_xg = jnp.concatenate([rows_x, rows_g], axis=0)
    xg_c = send(rows_xg, flip=1)
    rows = rows_f, rows_x, rows_g
    act_f, dpre = call(
        own_kernel, "own", [shape(count, 2 * hidden)] * 2, (*rows, up_in, down_in, up_c, down_c), cost(2, 12)
    )
    part_f, part_b = call(
        near_kernel,
        "near",
        [shape(count, width, dtype=F32)] * 2,
        (*rows, act_f, dpre, up_in, down_in, up_c, down_c, up_y, down_y),
        cost(3, 18),
    )
    outs = call(
        lambda *refs: far_kernel(cap, joined, *refs),
        "far",
        [shape(each, width)] * experts if joined else [shape(cap, width)] * (2 * experts),
        (*after(rows, xg_c), part_f, part_b, up_d, down_d),
        cost(2, 10),
    )

    shift = 1
    split = 4 * each // 10 // 8 * 8
    ways = range(len(outs))

    def back(value, i):
        return send(value, planes=-(i % experts), pipes=1 if i < experts else -1)

    ret = [back(outs[i][:split] if i % experts == shift else outs[i], i) for i in ways]
    ret_late = after([outs[i][split:] for i in ways if i % experts == shift], *ret)
    ret_late = [back(part, i * experts + shift) for i, part in enumerate(ret_late)]

    xg_y = send(*after([rows_xg], up_y, down_y), flip=2)
    chip_up, chip_down = call(
        chip_grads_kernel,
        "chip_grads",
        [shape(width, hidden, dtype=F32), shape(hidden, width, dtype=F32)],
        (rows_xg, xg_c, up_in, down_in),
        cost(2, 10),
        limit=12,
    )
    xg_d = send(*after([xg_y], chip_up, chip_down, *ret), flip=1)
    tables = [base_b[:, width:]] if joined else [table_f, base_b[:, width:]]
    bases = [(res_f, base_b)] if joined else [(res_f,), (base_b,)]
    totals = []
    for i, (base, table) in enumerate(zip(bases, tables)):
        totals += call(
            lambda *refs: combine_first_kernel(each, len(base), *refs),
            "combine_first",
            [shape(len(base) * tok_rows, width, dtype=F32)],
            (table, *base, *ret[i * experts:(i + 1) * experts]),
            cost(0.2, 4),
        )
    xg_d, *totals = after([xg_d, *totals])
    tiles = width // (2 * hidden)
    grad_up, grad_down = call(
        grads_kernel,
        "grads",
        [shape(width, hidden, dtype=F32), shape(hidden, width, dtype=F32)],
        (xg_y, xg_d, up_in, down_in, chip_up, chip_down),
        cost(0.01, 0.1),
        limit=16,
        out_specs=[HBM] * 2,
        scratch_shapes=[
            pltpu.VMEM((width, hidden), F32), pltpu.VMEM((hidden, width), F32), pltpu.SemaphoreType.DMA((2, tiles)),
        ],
    )

    tables = after(tables, grad_up, grad_down)
    results = []
    for i, (table, total) in enumerate(zip(tables, totals)):
        results += call(
            lambda *refs: combine_kernel(experts, each, shift * each + split, *refs),
            "combine",
            [shape(tok_rows, width)] * len(bases[i]),
            (table, total, ret_late[i]),
            cost(0.1, 3),
        )
    fwd_next, back_next = results
    return (fwd_next[None], back_next[None], grad_up[None, None], grad_down[None, None])


def solution(mesh):
    rows = P("pipe", "expert", None)
    slices = P("pipe", "expert", None, None)
    return jax.shard_map(
        local,
        mesh=mesh,
        in_specs=(rows,) * 7 + (slices,) * 2,
        out_specs=(rows, rows, slices, slices),
        check_vma=False,
    )
```

```python
import jax
import jax.numpy as jnp
from jax import lax
from jax.experimental import pallas as pl
from jax.experimental.pallas import tpu as pltpu
from jax.sharding import PartitionSpec as P

GROUP = 4
LANES = 128
F32 = jnp.float32
BF16 = jnp.bfloat16
VMEM = pl.BlockSpec(memory_space=pltpu.VMEM)
SMEM = pl.BlockSpec(memory_space=pltpu.SMEM)
HBM = pl.BlockSpec(memory_space=pltpu.HBM)


def after(values, *before):
    return list(lax.optimization_barrier((tuple(values), before))[0])


def dot(left, right, contract):
    return lax.dot_general(left, right, ((contract[:1], contract[1:]), ((), ())), preferred_element_type=F32)


def shape(*dims, dtype=BF16):
    return jax.ShapeDtypeStruct(dims, dtype)


def cost(gflops, mib):
    return pl.CostEstimate(flops=int(gflops * 1e9), bytes_accessed=int(mib * 2**20), transcendentals=0)


def start_copies(pairs, sems):
    copies = [pltpu.make_async_copy(src, dst, sems.at[i]) for i, (src, dst) in enumerate(pairs)]
    for copy in copies:
        copy.start()
    return copies


def build_kernel(
    experts, cap, joined, mine_ref, fr_ref, fg_ref, br_ref, bg_ref, f_any, x_any, g_any, *refs
):
    (f_ref, x_ref, g_ref, sems), refs = refs[-4:], refs[:-4]
    targets, held = refs[:len(refs) // 2], refs[len(refs) // 2:]
    outs, base_b, more = held[:experts], held[experts], held[experts + 1:]
    copies = start_copies(((f_any, f_ref), (x_any, x_ref), (g_any, g_ref)), sems)
    leaving = [pltpu.make_async_copy(src, dst, sems.at[3 + i]) for i, (src, dst) in enumerate(zip(held, targets))]
    tok_rows = f_ref.shape[0]
    wide = table_width(experts, 2 * cap if joined else cap)
    mine = mine_ref[0]
    row = lax.broadcasted_iota(jnp.int32, (tok_rows, tok_rows), 0)
    col = lax.broadcasted_iota(jnp.int32, (tok_rows, tok_rows), 1)
    earlier = (row < col).astype(F32).astype(BF16)
    same = (row == col).astype(F32).astype(BF16)
    slot = lax.broadcasted_iota(jnp.int32, (cap, tok_rows), 0).astype(F32)
    at = [lax.rem(mine + k, experts) for k in range(experts)]

    def placed(routes, gates):
        named = [((routes[0:1] == e) | (routes[1:2] == e)).astype(F32) for e in at]
        gate = [jnp.where(routes[0:1] == e, gates[0:1], gates[1:2]) for e in at]
        rows = -(-experts // 16) * 16
        padded = jnp.concatenate(named + [jnp.zeros((rows - experts, tok_rows), F32)], axis=0)
        prefix = dot(padded.astype(BF16), earlier, (1, 0))
        hits = [jnp.where(prefix[k:k + 1] == slot, named[k], 0.0) for k in range(experts)]
        return hits, [hits[k] * gate[k] for k in range(experts)]

    def by_token(slots):
        filled = sum(part.shape[0] for part in slots)
        full = jnp.concatenate(slots + [jnp.zeros((wide - filled, tok_rows), F32)], axis=0)
        return dot(same, full.astype(BF16), (1, 1)).astype(BF16)

    hits_f, gated_f = placed(fr_ref[...], fg_ref[...])
    hits_b, gated_b = placed(br_ref[...], bg_ref[...])
    rest_f = [part - part.astype(BF16).astype(F32) for part in gated_f]
    empty = jnp.zeros((cap, tok_rows), F32)
    for copy in copies:
        copy.wait()
    for k in range(experts):
        hits = hits_b[k].astype(BF16)
        rows_f = dot(hits_f[k].astype(BF16), f_ref[...], (1, 0))
        rows_x = dot(hits, x_ref[...], (1, 0))
        rows_g = dot(hits, g_ref[...], (1, 0)) * jnp.sum(gated_b[k], axis=1, keepdims=True)
        outs[k][...] = jnp.concatenate([rows_f, rows_x, rows_g], axis=0).astype(BF16)
        leaving[k].start()

    width = f_ref.shape[1]
    base_b[:, :width] = g_ref[...]
    tables = [gated_f, rest_f]
    if joined:
        tables[0] = [part for k in range(experts) for part in (gated_f[k], hits_b[k])]
        tables[1] = [part for k in range(experts) for part in (rest_f[k], empty)]
    else:
        base_b[:, width:] = by_token(hits_b)
    for i, part in enumerate(tables):
        low = i * wide
        if joined:
            base_b[:, width + low:width + low + wide] = by_token(part)
        else:
            more[0][:, low:low + wide] = by_token(part)
    for copy in leaving[experts:]:
        copy.start()
    for copy in leaving:
        copy.wait()


def table_width(experts, each):
    return -(-experts * each // LANES) * LANES


def stage_kernel(*refs):
    half = len(refs) // 2
    for copy in start_copies(zip(refs[:half], refs[half:-1]), refs[-1]):
        copy.wait()


def silu_slope(pre):
    sigma = 1.0 / (1.0 + jnp.exp(-pre))
    return pre * sigma, sigma * (1.0 + pre * (1.0 - sigma))


def hidden_units(rows_f, rows_x, rows_g, weights):
    count = rows_f.shape[0]
    up, down = weights
    pre = dot(jnp.concatenate([rows_f[...], rows_x[...]], axis=0), up[...], (1, 0))
    act, slope = silu_slope(pre)
    dact = dot(rows_g[...], down[...], (1, 1))
    return act[:count].astype(BF16), (dact * slope[count:]).astype(BF16)


def own_kernel(rows_f, rows_x, rows_g, up, down, up_c, down_c, act_f, dpre):
    side = down.shape[0]
    for q, weights in enumerate(((up, down), (up_c, down_c))):
        cols = slice(q * side, (q + 1) * side)
        act_f[:, cols], dpre[:, cols] = hidden_units(rows_f, rows_x, rows_g, weights)


def near_kernel(rows_f, rows_x, rows_g, act_f, dpre, up, down, up_c, down_c, up_y, down_y, part_f, part_b):
    side = down.shape[0]
    last_act, last_dpre = hidden_units(rows_f, rows_x, rows_g, (up_y, down_y))
    acts = [act_f[:, :side], act_f[:, side:], last_act]
    dpres = [dpre[:, :side], dpre[:, side:], last_dpre]
    for j in range(0, part_f.shape[1], side):
        cols = slice(j, j + side)
        part_f[:, cols] = sum(dot(a, w[:, cols], (1, 0)) for a, w in zip(acts, (down, down_c, down_y)))
        part_b[:, cols] = sum(dot(d, w[cols, :], (1, 1)) for d, w in zip(dpres, (up, up_c, up_y)))


def far_kernel(cap, joined, rows_f, rows_x, rows_g, part_f, part_b, up, down, *outs):
    side = down.shape[0]
    act_f, dpre = hidden_units(rows_f, rows_x, rows_g, (up, down))
    experts = rows_f.shape[0] // cap
    for j in range(0, part_f.shape[1], side):
        cols = slice(j, j + side)
        out_f = part_f[:, cols] + dot(act_f, down[:, cols], (1, 0))
        out_b = part_b[:, cols] + dot(dpre, up[cols, :], (1, 1))
        for k in range(experts):
            rows = slice(k * cap, (k + 1) * cap)
            if joined:
                outs[k][:, cols] = jnp.concatenate([out_f[rows], out_b[rows]], axis=0).astype(BF16)
            else:
                outs[k][:, cols] = out_f[rows].astype(BF16)
                outs[experts + k][:, cols] = out_b[rows].astype(BF16)


def group_units(pieces, up, down):
    count = pieces[0].shape[0] // 2
    acts, dpres = [], []
    for piece in pieces:
        act, slope = silu_slope(dot(piece[:count], up[...], (1, 0)))
        dact = dot(piece[count:], down[...], (1, 1))
        acts.append(act.astype(BF16))
        dpres.append((dact * slope).astype(BF16))
    return jnp.concatenate(acts, axis=0), jnp.concatenate(dpres, axis=0)


def group_columns(pieces, cols):
    count = pieces[0].shape[0] // 2
    return [jnp.concatenate([piece[low:low + count, cols] for piece in pieces], axis=0) for low in (0, count)]


def chip_grads_kernel(xg_own, xg_c, own_up, own_down, up, down):
    pieces = (xg_own, xg_c)
    act, dpre = group_units(pieces, own_up, own_down)
    side, width = down.shape
    for low in range(0, width, 2 * side):
        cols = slice(low, low + 2 * side)
        rows_x, rows_g = group_columns(pieces, cols)
        up[cols, :] = dot(rows_x, dpre, (0, 0))
        down[:, cols] = dot(act, rows_g, (0, 0))


def grads_kernel(xg_y, xg_d, own_up, own_down, chip_up, chip_down, grad_up, grad_down, up, down, sems):
    pieces = (xg_y, xg_d)
    act, dpre = group_units(pieces, own_up, own_down)
    side, width = down.shape
    copies = []
    for t, low in enumerate(range(0, width, 2 * side)):
        cols = slice(low, low + 2 * side)
        rows_x, rows_g = group_columns(pieces, cols)
        up[cols, :] = chip_up[cols, :] + dot(rows_x, dpre, (0, 0))
        down[:, cols] = chip_down[:, cols] + dot(act, rows_g, (0, 0))
        span = pl.ds(low, 2 * side)
        copies.append(pltpu.make_async_copy(up.at[span], grad_up.at[span], sems.at[0, t]))
        copies.append(pltpu.make_async_copy(down.at[:, span], grad_down.at[:, span], sems.at[1, t]))
        copies[-2].start()
        copies[-1].start()
    for copy in copies:
        copy.wait()


def picked_rows(experts, each, count, table, pieces, cols):
    tokens, wide = table.shape[0], table_width(experts, each)
    parts = [table[:, low:low + wide] for low in range(0, table.shape[1], wide)]
    if count == 2:
        forth = lax.broadcasted_iota(jnp.int32, (tokens, wide), 1) % each < each // 2
        parts = [jnp.where(forth, parts[0], 0), jnp.where(forth, 0, parts[0]), parts[1]]
    tables = jnp.concatenate(parts, axis=0)
    picked = sum(dot(tables[:, at:at + part.shape[0]], part[:, cols], (1, 0)) for at, part in pieces)
    total = picked[:count * tokens]
    if len(parts) > count:
        low = [picked[count * tokens:]]
        total = total + jnp.concatenate(low + [jnp.zeros((tokens, low[0].shape[1]), F32)] * (count - 1), axis=0)
    return total


def combine_first_kernel(each, count, table, *refs):
    base, whole, out = refs[:count], refs[count:-1], refs[-1]
    rows, width = base[0].shape[0], out.shape[1]
    pieces = [(k * each, part) for k, part in enumerate(whole)]
    for low in range(0, width, width // 7):
        cols = slice(low, low + width // 7)
        picked = picked_rows(len(whole), each, count, table, pieces, cols)
        for i in range(count):
            span = slice(i * rows, (i + 1) * rows)
            out[span, cols] = base[i][:, cols].astype(F32) + picked[span]


def combine_kernel(experts, each, at, table, total, late, *outs):
    rows, width = outs[0].shape
    for low in range(0, width, width // 7):
        cols = slice(low, low + width // 7)
        picked = total[:, cols] + picked_rows(experts, each, len(outs), table, [(at, late)], cols)
        for i, out in enumerate(outs):
            out[:, cols] = picked[i * rows:(i + 1) * rows].astype(BF16)


def local(
    fwd_acts, fwd_routes, fwd_gates, back_acts, back_routes, back_gates, back_grads, w_up, w_down
):
    devices = lax.axis_size("expert")
    sections = lax.axis_size("pipe")
    experts = devices // GROUP
    tok_rows, width = fwd_acts.shape[1:]
    cap = GROUP * (5 * tok_rows * fwd_routes.shape[2] // (4 * devices))
    mine = lax.axis_index("expert") // GROUP
    hidden = w_up.shape[3]
    count = experts * cap
    joined = sections == 2
    each = 2 * cap if joined else cap
    wide = table_width(experts, each)

    def send(value, planes=0, flip=0, pipes=0):
        pairs = []
        for section in range(sections):
            for place in range(devices):
                target = (place // GROUP + planes) % experts * GROUP + (place % GROUP ^ flip)
                goal = (section + pipes) % sections * devices + target
                pairs.append((section * devices + place, goal))
        return lax.ppermute(value, ("pipe", "expert"), pairs)

    def call(kernel, name, out_shape, inputs, estimate, limit=8, **more):
        return pl.pallas_call(
            kernel,
            out_shape=out_shape,
            in_specs=more.pop("in_specs", [VMEM] * len(inputs)),
            out_specs=more.pop("out_specs", [VMEM] * len(out_shape)),
            name=name,
            compiler_params=pltpu.CompilerParams(vmem_limit_bytes=limit * 2**20),
            cost_estimate=estimate,
            **more,
        )(*inputs)

    fwd_input, back_input, out_grad = fwd_acts[0], back_acts[0], back_grads[0]
    away = range(1, experts)

    up_own, down_own = w_up[0, 0], w_down[0, 0]
    up_c, down_c = send(up_own, flip=1), send(down_own, flip=1)
    res_f = send(fwd_input, pipes=1)
    tables = [shape(tok_rows, width + 2 * wide)]
    if not joined:
        tables = [shape(tok_rows, width + wide), shape(tok_rows, 2 * wide)]
    leaving = [shape(3 * cap, width)] * experts + tables
    built = call(
        lambda *refs: build_kernel(experts, cap, joined, *refs),
        "build",
        leaving,
        (
            mine.reshape(1), fwd_routes[0].T, fwd_gates[0].T, back_routes[0].T, back_gates[0].T,
            fwd_input, back_input, out_grad,
        ),
        cost(100, 0.1),
        limit=56,
        in_specs=[SMEM] + [VMEM] * 4 + [HBM] * 3,
        out_specs=[HBM] * len(leaving),
        scratch_shapes=[pltpu.VMEM(part.shape, BF16) for part in leaving]
        + [pltpu.VMEM((tok_rows, width), BF16)] * 3
        + [pltpu.SemaphoreType.DMA((3 + len(leaving),))],
    )
    got, tables = list(built[:experts]), built[experts:]

    up_sent, down_sent = after([up_own, down_own], tables[0])
    up_y, down_y = send(up_sent, flip=2), send(down_sent, flip=2)
    base_b = send(tables[0], pipes=-1)
    table_f = None if joined else send(tables[1], pipes=1)
    got[1:] = after(got[1:], up_c, down_c)
    got[1:-1] = [send(part, planes=k) for k, part in enumerate(got[1:-1], 1)]
    up_in, down_in, down_c = call(
        stage_kernel, "stage",
        [shape(width, hidden), shape(hidden, width), shape(hidden, width)],
        (up_own, down_own, down_c),
        cost(0.01, 0.1),
        limit=4,
        in_specs=[HBM] * 3,
        scratch_shapes=[pltpu.SemaphoreType.DMA((3,))],
    )
    got[-1] = send(*after([got[-1]], up_in, res_f), planes=experts - 1)
    up_d = send(up_y, flip=1)
    down_d = send(*after([down_y], up_in, base_b), flip=1)

    rows_f, rows_x, rows_g = (
        jnp.concatenate([part[i * cap:(i + 1) * cap] for part in got], axis=0) for i in range(3)
    )
    rows_xg = jnp.concatenate([rows_x, rows_g], axis=0)
    xg_c = send(rows_xg, flip=1)
    rows = rows_f, rows_x, rows_g
    act_f, dpre = call(
        own_kernel, "own", [shape(count, 2 * hidden)] * 2, (*rows, up_in, down_in, up_c, down_c), cost(2, 12)
    )
    part_f, part_b = call(
        near_kernel,
        "near",
        [shape(count, width, dtype=F32)] * 2,
        (*rows, act_f, dpre, up_in, down_in, up_c, down_c, up_y, down_y),
        cost(3, 18),
    )
    outs = call(
        lambda *refs: far_kernel(cap, joined, *refs),
        "far",
        [shape(each, width)] * experts if joined else [shape(cap, width)] * (2 * experts),
        (*after(rows, xg_c), part_f, part_b, up_d, down_d),
        cost(2, 10),
    )

    shift = 1
    split = 4 * each // 10 // 8 * 8
    ways = range(len(outs))

    def back(value, i):
        return send(value, planes=-(i % experts), pipes=1 if i < experts else -1)

    ret = [back(outs[i][:split] if i % experts == shift else outs[i], i) for i in ways]
    ret_late = after([outs[i][split:] for i in ways if i % experts == shift], *ret)
    ret_late = [back(part, i * experts + shift) for i, part in enumerate(ret_late)]

    xg_y = send(*after([rows_xg], up_y, down_y), flip=2)
    chip_up, chip_down = call(
        chip_grads_kernel,
        "chip_grads",
        [shape(width, hidden, dtype=F32), shape(hidden, width, dtype=F32)],
        (rows_xg, xg_c, up_in, down_in),
        cost(2, 10),
        limit=12,
    )
    xg_d = send(*after([xg_y], chip_up, chip_down, *ret), flip=1)
    tables = [base_b[:, width:]] if joined else [table_f, base_b[:, width:]]
    bases = [(res_f, base_b)] if joined else [(res_f,), (base_b,)]
    totals = []
    for i, (base, table) in enumerate(zip(bases, tables)):
        totals += call(
            lambda *refs: combine_first_kernel(each, len(base), *refs),
            "combine_first",
            [shape(len(base) * tok_rows, width, dtype=F32)],
            (table, *base, *ret[i * experts:(i + 1) * experts]),
            cost(0.2, 4),
        )
    xg_d, *totals = after([xg_d, *totals])
    tiles = width // (2 * hidden)
    grad_up, grad_down = call(
        grads_kernel,
        "grads",
        [shape(width, hidden, dtype=F32), shape(hidden, width, dtype=F32)],
        (xg_y, xg_d, up_in, down_in, chip_up, chip_down),
        cost(0.01, 0.1),
        limit=16,
        out_specs=[HBM] * 2,
        scratch_shapes=[
            pltpu.VMEM((width, hidden), F32), pltpu.VMEM((hidden, width), F32), pltpu.SemaphoreType.DMA((2, tiles)),
        ],
    )

    tables = after(tables, grad_up, grad_down)
    results = []
    for i, (table, total) in enumerate(zip(tables, totals)):
        results += call(
            lambda *refs: combine_kernel(experts, each, shift * each + split, *refs),
            "combine",
            [shape(tok_rows, width)] * len(bases[i]),
            (table, total, ret_late[i]),
            cost(0.1, 3),
        )
    fwd_next, back_next = results
    return (fwd_next[None], back_next[None], grad_up[None, None], grad_down[None, None])


def solution(mesh):
    rows = P("pipe", "expert", None)
    slices = P("pipe", "expert", None, None)
    return jax.shard_map(
        local,
        mesh=mesh,
        in_specs=(rows,) * 7 + (slices,) * 2,
        out_specs=(rows, rows, slices, slices),
        check_vma=False,
    )
```
